512 devices in a mesh: section: 16 (over z), node: 32 (over y, x, core).
Axes of the slice: x: 4, y: 4, z: 16, core: 2. Of those that a mesh axis runs over, the one named last changes fastest.
Arguments:
- initial: bfloat16 [2, 16384, 256], P(None, 'node'), may hold values from -6 to 6
- adjacency: bfloat16 [2, 384, 128, 128], P(None, 'node'), may hold values from -0.5 to 0.5
- sources: int32 [2, 384], P(None, 'node'), may hold values from 0 to 5, as said below
- boundary_rows: int32 [2, 4096], P(None, 'node'), may hold values from 0 to 511, as said below
- boundary_count: int32 [2, 32], P(None, 'node'), may hold values from 32 to 128, as said below
- layer_weights: bfloat16 [16, 256, 256], P('section'), may hold values from -0.375 to 0.375
Outputs:
- section_out: bfloat16 [16, 2, 16384, 256], P('section', None, 'node')
The draws below stay inside these ranges and needn't reach their ends.
Inputs may be any that keep to these rules, and one draw needn't show every extreme that they name: `sources`: each aligned group of 3 entries names, in some order, one of the partition's own tiles 0 .. 3, tile 512 // 128 (the previous partition's boundary block) and tile 512 // 128 + 1 (the next one's). `boundary_rows`: the 128 entries of one partition are distinct rows of it. `boundary_count`: some partition of each span has a full block.
All inputs are finite; a program needn't handle non-finite values.
Results may differ from the reference program's by a relative error of at most 0.027.
Values may be sent and summed in bfloat16 or wider, within the bound.
A program may use at most 64 MiB of HBM per device.

```python
import jax
import jax.numpy as jnp

D = 256
LAYERS_SECTION = 1
LAYERS = 16
SPANS = 2
ROWS = 512
TILE = 128
NBR = 3
BND = 128
NT = 12
SHARDS = 32
NODES = 16384
N_SECTION = 16


def draw_sources(key, part):
    key = jax.random.fold_in(key, 11)
    first_key, second_key = jax.random.split(key)
    blocks = SPANS * SHARDS * (ROWS // TILE)
    own_tile = jax.random.randint(first_key, (blocks,), 0, ROWS // TILE)
    triple = jnp.stack([own_tile, jnp.full((blocks,), ROWS // TILE), jnp.full((blocks,), ROWS // TILE + 1)], axis=1)
    orders = jax.vmap(lambda subkey: jax.random.permutation(subkey, 3))(jax.random.split(second_key, blocks))
    chosen = jnp.take_along_axis(triple, orders, axis=1)
    return chosen.reshape(SPANS, SHARDS * NT).astype(jnp.int32)


def draw_boundary_rows(key, part):
    key = jax.random.fold_in(key, 23)
    picks = jax.vmap(lambda subkey: jax.random.permutation(subkey, ROWS)[:BND])(jax.random.split(key, SPANS * SHARDS))
    return picks.reshape(SPANS, SHARDS * BND).astype(jnp.int32)


def draw_boundary_count(key, part):
    key = jax.random.fold_in(key, 37)
    first_key, second_key = jax.random.split(key)
    counted = jax.random.randint(first_key, (SPANS, SHARDS), BND // 4, BND + 1)
    fullest = jax.random.randint(second_key, (SPANS,), 0, SHARDS)
    counted = jnp.where(jnp.arange(SHARDS)[None, :] == fullest[:, None], BND, counted)
    return counted.astype(jnp.int32)


def shard_levels(stream_key, dims, cuts, least, high):
    factor_of = 1.0
    for position, shards_of in cuts:
        heights = jax.random.uniform(jax.random.fold_in(jax.random.fold_in(stream_key, 6), position), (shards_of,), jnp.float32, least / len(cuts), high / len(cuts))
        factor_of = factor_of * jnp.repeat(jnp.exp(heights), dims[position] // shards_of).reshape((-1,) + (1,) * (len(dims) - 1 - position))
    return factor_of


def noise(rng, extent, width, bound, cuts=(), dtype=jnp.bfloat16):
    level = shard_levels(rng, extent, cuts, -0.22, 0.18) if cuts else 1.0
    result = jax.random.normal(rng, extent, jnp.float32) * width * level
    return jnp.minimum(jnp.maximum(result, -bound), bound).astype(dtype)


def setup_inputs(seed: int = 0) -> dict:
    streams_of = jax.random.split(jax.random.key(seed), 7)
    return {
        "initial": noise(streams_of[0], (SPANS, NODES, D), 1.0, 6.0, ((1, 32),)),
        "adjacency": noise(streams_of[1], (SPANS, SHARDS * NT, TILE, TILE), (NBR * TILE * 2 // 5) ** -0.5, 0.5, ((1, 32),)),
        "sources": draw_sources(jax.random.fold_in(streams_of[6], 71), 0),
        "boundary_rows": draw_boundary_rows(jax.random.fold_in(streams_of[6], 71), 0),
        "boundary_count": draw_boundary_count(jax.random.fold_in(streams_of[6], 71), 0),
        "layer_weights": noise(streams_of[5], (LAYERS, D, D), D ** -0.5, 0.375, ((0, 16),)),
    }


alpha_mix = 0.1
lambda_decay = 0.5


def gcn_layer(hidden, anchor, adjacency, sources, boundary_rows, boundary_count, weight, mixing):
    live_mask = (jnp.arange(BND)[None, :] < boundary_count[:, None]).astype(jnp.bfloat16)
    rim_rows = jnp.take_along_axis(hidden, boundary_rows[:, :, None], axis=1) * live_mask[:, :, None]
    preceding = jnp.roll(rim_rows, 1, axis=0)
    following = jnp.roll(rim_rows, -1, axis=0)
    source_pool = jnp.concatenate([hidden, preceding, following], axis=1)
    source_pool = source_pool.reshape(SHARDS, ROWS // TILE + 2, TILE, D)
    picked = jnp.take_along_axis(source_pool, sources[:, :, None, None], axis=1)
    products = jnp.einsum("sntk,snkd->sntd", adjacency.astype(jnp.float32), picked.astype(jnp.float32))
    aggregate = products.reshape(SHARDS, ROWS // TILE, NBR, TILE, D).sum(axis=2).reshape(SHARDS, ROWS, D)
    blended = (1.0 - alpha_mix) * aggregate + alpha_mix * anchor.astype(jnp.float32)
    blended_b = blended.astype(jnp.bfloat16).reshape(SHARDS * ROWS, D)
    projected = jnp.dot(blended_b, weight, preferred_element_type=jnp.float32).reshape(SHARDS, ROWS, D)
    return jax.nn.relu((1.0 - mixing) * blended + mixing * projected).astype(jnp.bfloat16)


def reference(initial, adjacency, sources, boundary_rows, boundary_count, layer_weights):
    results = []
    for span_number in range(SPANS):
        anchor = initial[span_number].reshape(SHARDS, ROWS, D)
        tile_weights = adjacency[span_number].reshape(SHARDS, NT, TILE, TILE)
        tile_sources = sources[span_number].reshape(SHARDS, NT)
        rim_index = boundary_rows[span_number].reshape(SHARDS, BND)
        rim_count = boundary_count[span_number]
        hidden = anchor
        per_section = []
        for section_number in range(N_SECTION):
            for inner in range(LAYERS_SECTION):
                layer_number = section_number * LAYERS_SECTION + inner
                mixing = jnp.log(lambda_decay / (jnp.float32(layer_number) + 1.0) + 1.0)
                hidden = gcn_layer(hidden, anchor, tile_weights, tile_sources, rim_index, rim_count, layer_weights[layer_number], mixing)
            per_section.append(hidden.reshape(NODES, D))
        results.append(jnp.stack(per_section))
    return jnp.stack(results, axis=1)
```

```python
import jax
import jax.numpy as jnp
import numpy as np
from jax import lax
from jax.experimental import pallas as pl
from jax.experimental.pallas import tpu as pltpu
from jax.sharding import PartitionSpec as P

MESH = pl.DeviceIdType.MESH

alpha_mix = 0.1
lambda_decay = 0.5

SPANS = 2
ROWS = 512
TILE = 128
WIDTH = 256
RIM = 128
OWN = ROWS // TILE
POOL = ROWS + 2 * RIM
CHUNK = 256


def dot(a, b):
    return jnp.dot(a, b, preferred_element_type=jnp.float32)


def layers_kernel(
    sections,
    shards,
    betas_ref,
    sources_ref,
    count_ref,
    rows_ref,
    initial_ref,
    adjacency_ref,
    weight_ref,
    out_ref,
    weights,
    pool,
    rims,
    full_adj,
    rim_adj,
    rim_send,
    rim_recv,
    down_send,
    down_recv,
    up_send,
    up_recv,
    side_send,
    side_recv,
    out_sem,
):
    z = lax.axis_index("section")
    p = lax.axis_index("node")
    core = lax.rem(p, 2)
    sibling = p + 1 - 2 * core
    before, after = lax.rem(p + shards - 1, shards), lax.rem(p + 1, shards)
    below, above = lax.rem(z + sections - 1, sections), lax.rem(z + 1, sections)
    down_steps = sections // 2
    up_steps = sections - 1 - down_steps

    barrier = pltpu.get_barrier_semaphore()
    for neighbour in ((z, before), (z, after), (below, p), (above, p)):
        pl.semaphore_signal(barrier, inc=1, device_id=neighbour, device_id_type=MESH)

    def down_copy(step):
        index = lax.rem(z + step - 1, sections)
        return pltpu.make_async_remote_copy(
            src_ref=weights.at[index, core],
            dst_ref=weights.at[index, core],
            send_sem=down_send.at[step - 1],
            recv_sem=down_recv.at[step - 1],
            device_id=(below, p),
            device_id_type=MESH,
        )

    def down_arrival(step):
        index = lax.rem(z + step, sections)
        return pltpu.make_async_remote_copy(
            src_ref=weights.at[index, core],
            dst_ref=weights.at[index, core],
            send_sem=down_send.at[step - 1],
            recv_sem=down_recv.at[step - 1],
            device_id=(below, p),
            device_id_type=MESH,
        )

    def up_copy(step):
        index = lax.rem(z - step + 1 + sections, sections)
        return pltpu.make_async_remote_copy(
            src_ref=weights.at[index, core],
            dst_ref=weights.at[index, core],
            send_sem=up_send.at[step - 1],
            recv_sem=up_recv.at[step - 1],
            device_id=(above, p),
            device_id_type=MESH,
        )

    def up_arrival(step):
        index = lax.rem(z - step + sections, sections)
        return pltpu.make_async_remote_copy(
            src_ref=weights.at[index, core],
            dst_ref=weights.at[index, core],
            send_sem=up_send.at[step - 1],
            recv_sem=up_recv.at[step - 1],
            device_id=(above, p),
            device_id_type=MESH,
        )

    def side_copy(index):
        return pltpu.make_async_remote_copy(
            src_ref=weights.at[index, core],
            dst_ref=weights.at[index, core],
            send_sem=side_send.at[index],
            recv_sem=side_recv.at[index],
            device_id=(z, sibling),
            device_id_type=MESH,
        )

    def side_arrival(index):
        return pltpu.make_async_remote_copy(
            src_ref=weights.at[index, core],
            dst_ref=weights.at[index, 1 - core],
            send_sem=side_send.at[index],
            recv_sem=side_recv.at[index],
            device_id=(z, sibling),
            device_id_type=MESH,
        )

    def relay(step):
        down_arrival(step).wait_recv()

        @pl.when(step < down_steps)
        def _():
            down_copy(step + 1).start()

        @pl.when(z + step >= sections)
        def _():
            side_copy(z + step - sections).start()

        @pl.when(step <= up_steps)
        def _():
            up_arrival(step).wait_recv()

            @pl.when(step < up_steps)
            def _():
                up_copy(step + 1).start()

            @pl.when(z - step >= 0)
            def _():
                side_copy(z - step).start()

    def rim_copies(layer, span):
        to_after = pltpu.make_async_remote_copy(
            src_ref=rims.at[layer, span],
            dst_ref=pool.at[layer, span, pl.ds(ROWS, RIM)],
            send_sem=rim_send.at[layer, span, 0],
            recv_sem=rim_recv.at[layer, span, 0],
            device_id=(z, after),
            device_id_type=MESH,
        )
        to_before = pltpu.make_async_remote_copy(
            src_ref=rims.at[layer, span],
            dst_ref=pool.at[layer, span, pl.ds(ROWS + RIM, RIM)],
            send_sem=rim_send.at[layer, span, 1],
            recv_sem=rim_recv.at[layer, span, 1],
            device_id=(z, before),
            device_id_type=MESH,
        )
        return to_after, to_before

    weights[z] = weight_ref[0].reshape(2, WIDTH // 2, WIDTH)

    lane = lax.broadcasted_iota(jnp.int32, (RIM, TILE), 1)
    row = lax.broadcasted_iota(jnp.int32, (RIM, TILE), 0)
    picks = []
    for span in range(SPANS):
        wanted = jnp.broadcast_to(rows_ref[span : span + 1, :], (RIM, RIM)).T
        wanted = jnp.where(row < count_ref[span, 0], wanted, -1)
        pick = jnp.concatenate(
            [jnp.where(wanted == lane + t * TILE, 1.0, 0.0) for t in range(OWN)], axis=1
        ).astype(jnp.bfloat16)
        picks.append(pick)
        rims[0, span] = dot(pick, initial_ref[span]).astype(jnp.bfloat16)

    pl.semaphore_wait(barrier, 4)
    for span in range(SPANS):
        for copy in rim_copies(0, span):
            copy.start()
    down_copy(1).start()
    up_copy(1).start()

    for span in range(SPANS):
        pool[0, span, pl.ds(0, ROWS)] = initial_ref[span]
        for block in range(OWN):
            first = sources_ref[span, 3 * block]
            second = sources_ref[span, 3 * block + 1]
            third = sources_ref[span, 3 * block + 2]
            at_before = jnp.where(second == OWN, 1, 0) + jnp.where(third == OWN, 2, 0)
            at_after = jnp.where(second == OWN + 1, 1, 0) + jnp.where(third == OWN + 1, 2, 0)
            at_own = jnp.minimum(3 - at_before - at_after, 2)
            own_tile = first + second + third - (2 * OWN + 1)
            place = pl.ds(block * TILE, TILE)
            own = adjacency_ref[span, 3 * block + at_own]
            for t in range(OWN):
                full_adj[span, place, t * TILE : (t + 1) * TILE] = jnp.where(
                    own_tile == t, own, jnp.zeros_like(own)
                )
            full_adj[span, place, ROWS : ROWS + RIM] = adjacency_ref[span, 3 * block + at_before]
            full_adj[span, place, ROWS + RIM : POOL] = adjacency_ref[span, 3 * block + at_after]
        rim_adj[span] = dot(picks[span], full_adj[span]).astype(jnp.bfloat16)

    def finish(aggregate, anchor, weight, mixing):
        blended = (1.0 - alpha_mix) * aggregate + alpha_mix * anchor.astype(jnp.float32)
        projected = dot(blended.astype(jnp.bfloat16), weight)
        return jnp.maximum((1.0 - mixing) * blended + mixing * projected, 0.0).astype(jnp.bfloat16)

    def all_rows(layer, span, mixing):
        weight = weights[layer].reshape(WIDTH, WIDTH)
        for start in range(0, ROWS, CHUNK):
            place = pl.ds(start, CHUNK)
            aggregate = dot(full_adj[span, place, :], pool[layer, span])
            pool[layer + 1, span, place] = finish(
                aggregate, initial_ref[span, place], weight, mixing
            )

    first_steps = jnp.minimum(sections - z, down_steps)
    lax.fori_loop(1, first_steps + 1, lambda step, c: (relay(step), c)[1], 0)

    def layer_step(layer, carry):
        mixing = betas_ref[layer]
        step = sections - z + layer

        @pl.when((layer >= 1) & (step <= down_steps))
        def _():
            relay(step)

        @pl.when(layer < z)
        def _():
            side_arrival(layer).wait_recv()

        for span in range(SPANS):
            own_part = dot(rim_adj[span, :, 0:ROWS], pool[layer, span, pl.ds(0, ROWS)])
            for copy in rim_copies(layer, span):
                copy.wait_recv()

            @pl.when(layer < z)
            def _():
                aggregate = own_part + dot(
                    rim_adj[span, :, ROWS:POOL], pool[layer, span, pl.ds(ROWS, 2 * RIM)]
                )
                weight = weights[layer].reshape(WIDTH, WIDTH)
                rims[layer + 1, span] = finish(aggregate, rims[0, span], weight, mixing)
                for copy in rim_copies(layer + 1, span):
                    copy.start()

        for span in range(SPANS):
            all_rows(layer, span, mixing)
            for copy in rim_copies(layer, span):
                copy.wait_send()
        return carry

    lax.fori_loop(0, z + 1, layer_step, 0)

    outs = [
        pltpu.make_async_copy(
            pool.at[z + 1, span, pl.ds(0, ROWS)], out_ref.at[0, span], out_sem.at[span]
        )
        for span in range(SPANS)
    ]
    for copy in outs:
        copy.start()

    lax.fori_loop(1, down_steps + 1, lambda step, c: (down_copy(step).wait_send(), c)[1], 0)
    lax.fori_loop(1, up_steps + 1, lambda step, c: (up_copy(step).wait_send(), c)[1], 0)
    lax.fori_loop(0, z, lambda index, c: (side_copy(index).wait_send(), c)[1], 0)
    for copy in outs:
        copy.wait()


def solution(mesh):
    sections, shards = mesh.shape["section"], mesh.shape["node"]
    ordinals = np.arange(sections, dtype=np.float32)
    betas = np.log(np.float32(lambda_decay) / (ordinals + np.float32(1.0)) + np.float32(1.0))

    def on_device(initial, adjacency, sources, boundary_rows, boundary_count, layer_weights):
        def body(*refs):
            layers_kernel(sections, shards, *refs)

        down_steps = sections // 2
        smem = pl.BlockSpec(memory_space=pltpu.SMEM)
        vmem = pl.BlockSpec(memory_space=pltpu.VMEM)
        dma = pltpu.SemaphoreType.DMA
        return pl.pallas_call(
            body,
            out_shape=jax.ShapeDtypeStruct((1, SPANS, ROWS, WIDTH), jnp.bfloat16),
            in_specs=[smem, smem, smem, vmem, vmem, vmem, vmem],
            out_specs=pl.BlockSpec(memory_space=pl.ANY),
            scratch_shapes=[
                pltpu.VMEM((sections, 2, WIDTH // 2, WIDTH), jnp.bfloat16),
                pltpu.VMEM((sections + 1, SPANS, POOL, WIDTH), jnp.bfloat16),
                pltpu.VMEM((sections, SPANS, RIM, WIDTH), jnp.bfloat16),
                pltpu.VMEM((SPANS, ROWS, POOL), jnp.bfloat16),
                pltpu.VMEM((SPANS, RIM, POOL), jnp.bfloat16),
                dma((sections, SPANS, 2)),
                dma((sections, SPANS, 2)),
                dma((down_steps,)),
                dma((down_steps,)),
                dma((down_steps,)),
                dma((down_steps,)),
                dma((sections,)),
                dma((sections,)),
                dma((SPANS,)),
            ],
            compiler_params=pltpu.CompilerParams(
                collective_id=0, has_side_effects=True, vmem_limit_bytes=48 * 1024 * 1024
            ),
        )(
            jnp.asarray(betas, jnp.float32),
            sources,
            boundary_count,
            boundary_rows,
            initial,
            adjacency,
            layer_weights,
        )

    in_specs = (
        P(None, "node", None),
        P(None, "node", None, None),
        P(None, "node"),
        P(None, "node"),
        P(None, "node"),
        P("section", None, None),
    )
    out_specs = P("section", None, "node", None)
    return jax.shard_map(
        on_device, mesh=mesh, in_specs=in_specs, out_specs=out_specs, check_vma=False
    )
```

```python
import jax
import jax.numpy as jnp
import numpy as np
from jax import lax
from jax.experimental import pallas as pl
from jax.experimental.pallas import tpu as pltpu
from jax.sharding import PartitionSpec as P

MESH = pl.DeviceIdType.MESH

alpha_mix = 0.1
lambda_decay = 0.5

SPANS = 2
ROWS = 512
TILE = 128
WIDTH = 256
RIM = 128
OWN = ROWS // TILE
POOL = ROWS + 2 * RIM
PIECES = 4
PIECE = WIDTH // PIECES
NOTES = 24
AHEAD = 3

ALL = pl.ds(0, ROWS)
FAR = pl.ds(ROWS, RIM)
NEAR = pl.ds(ROWS + RIM, RIM)
EDGES = pl.ds(ROWS, 2 * RIM)


def dot(a, b):
    return jnp.dot(a, b, preferred_element_type=jnp.float32)


def layers_kernel(
    sections,
    shards,
    row_shards,
    betas_ref,
    sources_ref,
    count_ref,
    rows_ref,
    initial_ref,
    adjacency_ref,
    weight_ref,
    out_ref,
    weights,
    pool,
    wide,
    edge,
    tight,
    notes,
    rim_wide,
    rim_edge,
    early,
    ship_send,
    ship_recv,
    rim_send,
    rim_recv,
    direct_send,
    direct_recv,
    share_send,
    share_recv,
    out_send,
    out_recv,
):
    z = lax.axis_index("section")
    p = lax.axis_index("node")
    span = lax.rem(z, 2)
    core = lax.rem(p, 2)
    shadow = lax.rem(p - 1 + 2 * core + shards, shards)
    sibling = p + 1 - 2 * core
    far_to = lax.rem(p + 2 - 4 * core + shards, shards)
    far_from = lax.rem(p - 2 + 4 * core + shards, shards)
    half = lax.rem(p // row_shards, 2)
    beside = p + row_shards - 2 * row_shards * half
    beside_sibling = beside + 1 - 2 * core
    piece = 2 * half + core
    others = (
        (sibling, 2 * half + 1 - core),
        (beside, 2 * (1 - half) + core),
        (beside_sibling, 2 * (1 - half) + 1 - core),
    )
    pair = z + 1 - 2 * span
    layers = z + 2 - span

    barrier = pltpu.get_barrier_semaphore()
    for node in (sibling, far_to, far_from, shadow, beside, beside_sibling):
        pl.semaphore_signal(barrier, inc=1, device_id=(z, node), device_id_type=MESH)

    def greet(step, carry):
        there = lax.rem(z + step, sections)
        pl.semaphore_signal(barrier, inc=1, device_id=(there, p), device_id_type=MESH)
        return carry

    lax.fori_loop(1, sections, greet, 0)

    def remote(src, dst, send, recv, device):
        return pltpu.make_async_remote_copy(
            src_ref=src,
            dst_ref=dst,
            send_sem=send,
            recv_sem=recv,
            device_id=device,
            device_id_type=MESH,
        )

    def ship(item):
        refs = (
            (notes.at[0], notes.at[1]),
            (pool.at[0, 0, ALL], pool.at[0, 1, ALL]),
            (tight.at[0], tight.at[1]),
            (edge.at[0], edge.at[1]),
        )[item]
        return remote(*refs, ship_send.at[item], ship_recv.at[item], (z, shadow))

    def rim_to_sibling(layer):
        return remote(
            pool.at[layer, 1, NEAR],
            pool.at[layer, 0, FAR],
            rim_send.at[layer, 0],
            rim_recv.at[layer, 0],
            (z, sibling),
        )

    def rim_to_far(layer):
        return remote(
            pool.at[layer, 1, NEAR],
            pool.at[layer, 1, FAR],
            rim_send.at[layer, 1],
            rim_recv.at[layer, 1],
            (z, far_to),
        )

    def direct(there):
        return remote(
            weights.at[z, piece],
            weights.at[z, piece],
            direct_send.at[there],
            direct_recv.at[z],
            (there, p),
        )

    def wants(there):
        return (there != z) & (there + 1 - lax.rem(there, 2) >= z)

    def share(layer, member):
        return remote(
            weights.at[layer, piece],
            weights.at[layer, piece],
            share_send.at[layer, member],
            share_recv.at[layer, piece],
            (z, others[member][0]),
        )

    def pass_on(layer):
        @pl.when((layer < layers) & (layer != z))
        def _():
            remote(
                weights.at[layer, piece],
                weights.at[layer, piece],
                direct_send.at[layer],
                direct_recv.at[layer],
                (pair, p),
            ).wait_recv()
            for member in range(PIECES - 1):
                share(layer, member).start()

    def have_weight(layer):
        @pl.when(layer != z)
        def _():
            for member in range(PIECES - 1):
                index = others[member][1]
                remote(
                    weights.at[layer, piece],
                    weights.at[layer, index],
                    share_send.at[layer, member],
                    share_recv.at[layer, index],
                    (z, sibling),
                ).wait_recv()

    def out_local():
        return pltpu.make_async_copy(pool.at[z + 1, 0, ALL], out_ref.at[0, span], out_send.at[0])

    def out_remote():
        return remote(
            pool.at[pair + 1, 0, ALL],
            out_ref.at[0, span],
            out_send.at[1],
            out_recv.at[0],
            (pair, p),
        )

    def out_arrival():
        return remote(
            pool.at[pair + 1, 0, ALL],
            out_ref.at[0, 1 - span],
            out_send.at[1],
            out_recv.at[0],
            (pair, p),
        )

    pool[0, 0, ALL] = initial_ref[span]
    weights[z] = weight_ref[0].reshape(PIECES, PIECE, WIDTH)
    wanted = jnp.where(span == 0, rows_ref[0:1, :], rows_ref[1:2, :])
    live = lax.broadcasted_iota(jnp.int32, (1, RIM), 1) < count_ref[span, 0]
    notes[0, 16:17, :] = jnp.where(live, wanted, -1).astype(jnp.float32)
    for block in range(OWN):
        first = sources_ref[span, 3 * block]
        second = sources_ref[span, 3 * block + 1]
        third = sources_ref[span, 3 * block + 2]
        at_before = jnp.where(second == OWN, 1, 0) + jnp.where(third == OWN, 2, 0)
        at_after = jnp.where(second == OWN + 1, 1, 0) + jnp.where(third == OWN + 1, 2, 0)
        at_own = jnp.minimum(3 - at_before - at_after, 2)
        own_tile = first + second + third - (2 * OWN + 1)
        place = pl.ds(block * TILE, TILE)
        at_far = jnp.where(core == 1, at_before, at_after)
        at_near = jnp.where(core == 1, at_after, at_before)
        edge[0, place, 0:RIM] = adjacency_ref[span, 3 * block + at_far]
        edge[0, place, RIM : 2 * RIM] = adjacency_ref[span, 3 * block + at_near]
        tight[0, place] = adjacency_ref[span, 3 * block + at_own]
        for t in range(OWN):
            chosen = jnp.where(own_tile == t, 1.0, 0.0)
            notes[0, 4 * block + t : 4 * block + t + 1, :] = jnp.full((1, TILE), chosen)

    lane = lax.broadcasted_iota(jnp.int32, (RIM, TILE), 1).astype(jnp.float32)

    def picker(unit):
        turned = jnp.broadcast_to(notes[unit, 16:17, :], (RIM, RIM)).T
        return jnp.concatenate(
            [jnp.where(turned == lane + float(t * TILE), 1.0, 0.0) for t in range(OWN)], axis=1
        ).astype(jnp.bfloat16)

    def first_rim(unit):
        pool[0, 1 - unit, NEAR] = dot(picker(unit), pool[0, unit, ALL]).astype(jnp.bfloat16)

    def spread(unit):
        pick = picker(unit)
        for block in range(OWN):
            place = pl.ds(block * TILE, TILE)
            own = tight[unit, place].astype(jnp.float32)
            for t in range(OWN):
                mask = notes[unit, 4 * block + t : 4 * block + t + 1, :]
                wide[unit, place, t * TILE : (t + 1) * TILE] = (own * mask).astype(jnp.bfloat16)
        rim_wide[unit] = dot(pick, wide[unit]).astype(jnp.bfloat16)
        rim_edge[unit] = dot(pick, edge[unit]).astype(jnp.bfloat16)

    def start_rim(unit, layer):
        early[unit] = dot(rim_wide[unit], pool[layer, unit, ALL])

    def finish(aggregate, anchor, layer):
        mixing = betas_ref[layer]
        blended = (1.0 - alpha_mix) * aggregate + alpha_mix * anchor.astype(jnp.float32)
        projected = dot(blended.astype(jnp.bfloat16), weights[layer].reshape(WIDTH, WIDTH))
        return jnp.maximum((1.0 - mixing) * blended + mixing * projected, 0.0).astype(jnp.bfloat16)

    def end_rim(unit, layer):
        aggregate = early[unit] + dot(rim_edge[unit], pool[layer, unit, EDGES])
        pool[layer + 1, 1 - unit, NEAR] = finish(aggregate, pool[0, 1 - unit, NEAR], layer)

    def all_rows(unit, layer):
        aggregate = dot(wide[unit], pool[layer, unit, ALL])
        aggregate += dot(edge[unit], pool[layer, unit, EDGES])
        pool[layer + 1, unit, ALL] = finish(aggregate, pool[0, unit, ALL], layer)

    first_rim(0)
    spread(0)
    pl.semaphore_wait(barrier, 6 + sections - 1)
    for item in range(4):
        ship(item).start()
    rim_to_sibling(0).start()
    rim_to_far(0).start()

    def send_weight(step, carry):
        there = sections - 1 - step

        @pl.when(wants(there))
        def _():
            direct(there).start()

        return carry

    lax.fori_loop(0, sections, send_weight, 0)

    start_rim(0, 0)
    ship(0).wait_recv()
    ship(1).wait_recv()
    first_rim(1)
    for layer in range(AHEAD):
        pass_on(layer)
    have_weight(0)
    rim_to_sibling(0).wait_recv()
    end_rim(0, 0)
    rim_to_sibling(1).start()

    @pl.when(layers > 2)
    def _():
        rim_to_far(1).start()

    all_rows(0, 0)
    start_rim(0, 1)
    ship(2).wait_recv()
    ship(3).wait_recv()
    spread(1)
    start_rim(1, 0)

    def step(i, carry):
        last = i == layers - 2

        @pl.when(last & (span == 0))
        def _():
            out_local().start()

        @pl.when(last & (span == 1))
        def _():
            out_remote().start()

        rim_to_far(i).wait_recv()
        end_rim(1, i)
        have_weight(i + 1)
        rim_to_sibling(i + 1).wait_recv()

        @pl.when(i < layers - 2)
        def _():
            end_rim(0, i + 1)
            rim_to_sibling(i + 2).start()

            @pl.when(i < layers - 3)
            def _():
                rim_to_far(i + 2).start()

            pass_on(i + AHEAD)
            all_rows(1, i)
            start_rim(1, i + 1)

        all_rows(0, i + 1)

        @pl.when(i < layers - 2)
        def _():
            start_rim(0, i + 2)

        return carry

    lax.fori_loop(0, layers - 1, step, 0)

    @pl.when(span == 1)
    def _():
        out_local().start()

    @pl.when(span == 0)
    def _():
        out_remote().start()

    for item in range(4):
        ship(item).wait_send()

    def sent(layer, carry):
        rim_to_sibling(layer).wait_send()

        @pl.when(layer < layers - 1)
        def _():
            rim_to_far(layer).wait_send()

        @pl.when(layer != z)
        def _():
            for member in range(PIECES - 1):
                share(layer, member).wait_send()

        return carry

    lax.fori_loop(0, layers, sent, 0)

    def sent_weight(there, carry):
        @pl.when(wants(there))
        def _():
            direct(there).wait_send()

        return carry

    lax.fori_loop(0, sections, sent_weight, 0)
    out_local().wait()
    out_remote().wait_send()
    out_arrival().wait_recv()


def solution(mesh):
    sections, shards = mesh.shape["section"], mesh.shape["node"]
    row_shards = 8 if shards >= 32 else 2
    ordinals = np.arange(sections, dtype=np.float32)
    betas = np.log(np.float32(lambda_decay) / (ordinals + np.float32(1.0)) + np.float32(1.0))

    def on_device(initial, adjacency, sources, boundary_rows, boundary_count, layer_weights):
        def body(*refs):
            layers_kernel(sections, shards, row_shards, *refs)

        smem = pl.BlockSpec(memory_space=pltpu.SMEM)
        vmem = pl.BlockSpec(memory_space=pltpu.VMEM)
        dma = pltpu.SemaphoreType.DMA
        return pl.pallas_call(
            body,
            out_shape=jax.ShapeDtypeStruct((1, SPANS, ROWS, WIDTH), jnp.bfloat16),
            in_specs=[smem, smem, smem, vmem, vmem, vmem, vmem],
            out_specs=pl.BlockSpec(memory_space=pl.ANY),
            scratch_shapes=[
                pltpu.VMEM((sections, PIECES, PIECE, WIDTH), jnp.bfloat16),
                pltpu.VMEM((sections + 1, 2, POOL, WIDTH), jnp.bfloat16),
                pltpu.VMEM((2, ROWS, ROWS), jnp.bfloat16),
                pltpu.VMEM((2, ROWS, 2 * RIM), jnp.bfloat16),
                pltpu.VMEM((2, ROWS, TILE), jnp.bfloat16),
                pltpu.VMEM((2, NOTES, TILE), jnp.float32),
                pltpu.VMEM((2, RIM, ROWS), jnp.bfloat16),
                pltpu.VMEM((2, RIM, 2 * RIM), jnp.bfloat16),
                pltpu.VMEM((2, RIM, WIDTH), jnp.float32),
                dma((4,)),
                dma((4,)),
                dma((sections, 2)),
                dma((sections, 2)),
                dma((sections,)),
                dma((sections,)),
                dma((sections, PIECES - 1)),
                dma((sections, PIECES)),
                dma((2,)),
                dma((1,)),
            ],
            compiler_params=pltpu.CompilerParams(
                collective_id=0, has_side_effects=True, vmem_limit_bytes=48 * 1024 * 1024
            ),
        )(
            jnp.asarray(betas, jnp.float32),
            sources,
            boundary_count,
            boundary_rows,
            initial,
            adjacency,
            layer_weights,
        )

    in_specs = (
        P(None, "node", None),
        P(None, "node", None, None),
        P(None, "node"),
        P(None, "node"),
        P(None, "node"),
        P("section", None, None),
    )
    out_specs = P("section", None, "node", None)
    return jax.shard_map(
        on_device, mesh=mesh, in_specs=in_specs, out_specs=out_specs, check_vma=False
    )
```

```python
import jax
import jax.numpy as jnp
import numpy as np
from jax import lax
from jax.experimental import pallas as pl
from jax.experimental.pallas import tpu as pltpu
from jax.sharding import PartitionSpec as P

MESH = pl.DeviceIdType.MESH

alpha_mix = 0.1
lambda_decay = 0.5

SPANS = 2
ROWS = 512
TILE = 128
WIDTH = 256
RIM = 128
OWN = ROWS // TILE
POOL = ROWS + 2 * RIM
PARTS = 2
PART = WIDTH // PARTS
NOTES = 24

ALL = pl.ds(0, ROWS)
FAR = pl.ds(ROWS, RIM)
NEAR = pl.ds(ROWS + RIM, RIM)
EDGES = pl.ds(ROWS, 2 * RIM)


def dot(a, b):
    return jnp.dot(a, b, preferred_element_type=jnp.float32)


def layers_kernel(
    sections,
    shards,
    initial_ref,
    adjacency_ref,
    sources_ref,
    rows_ref,
    count_ref,
    weight_ref,
    out_ref,
    betas,
    tiles,
    sources,
    rows,
    count,
    weights,
    pool,
    wide,
    edge,
    tight,
    notes,
    rim_wide,
    rim_edge,
    early,
    ship_send,
    ship_recv,
    rim_send,
    rim_recv,
    near_send,
    near_recv,
    down_send,
    down_recv,
    up_send,
    up_recv,
    side_send,
    side_recv,
    out_send,
    out_recv,
    in_sem,
):
    z = lax.axis_index("section")
    p = lax.axis_index("node")
    span = lax.rem(z, 2)
    core = lax.rem(p, 2)
    shadow = lax.rem(p - 1 + 2 * core + shards, shards)
    sibling = p + 1 - 2 * core
    far_to = lax.rem(p + 2 - 4 * core + shards, shards)
    far_from = lax.rem(p - 2 + 4 * core + shards, shards)
    below, above = lax.rem(z + sections - 1, sections), lax.rem(z + 1, sections)
    pair = z + 1 - 2 * span
    layers = z + 2 - span
    down_steps = sections // 2
    up_steps = sections - 1 - down_steps

    barrier = pltpu.get_barrier_semaphore()
    greeted = [(z, node) for node in (sibling, far_to, far_from, shadow)]
    greeted += [(below, p), (above, p)]
    for device in greeted:
        pl.semaphore_signal(barrier, inc=1, device_id=device, device_id_type=MESH)

    inputs = [
        pltpu.make_async_copy(src, dst, in_sem.at[index])
        for index, (src, dst) in enumerate(
            (
                (sources_ref, sources),
                (count_ref, count),
                (rows_ref, rows),
                (initial_ref.at[span], pool.at[0, 0, ALL]),
                (adjacency_ref.at[span], tiles),
                (weight_ref.at[0], weights.at[z]),
            )
        )
    ]
    for copy in inputs:
        copy.start()

    def remote(src, dst, send, recv, device):
        return pltpu.make_async_remote_copy(
            src_ref=src,
            dst_ref=dst,
            send_sem=send,
            recv_sem=recv,
            device_id=device,
            device_id_type=MESH,
        )

    def ship(item):
        refs = (
            (notes.at[0], notes.at[1]),
            (pool.at[0, 0, ALL], pool.at[0, 1, ALL]),
            (tight.at[0], tight.at[1]),
            (edge.at[0], edge.at[1]),
        )[item]
        return remote(*refs, ship_send.at[item], ship_recv.at[item], (z, shadow))

    def rim_to_sibling(layer):
        return remote(
            pool.at[layer, 1, NEAR],
            pool.at[layer, 0, FAR],
            rim_send.at[layer, 0],
            rim_recv.at[layer, 0],
            (z, sibling),
        )

    def rim_to_far(layer):
        return remote(
            pool.at[layer, 1, NEAR],
            pool.at[layer, 1, FAR],
            rim_send.at[layer, 1],
            rim_recv.at[layer, 1],
            (z, far_to),
        )

    def rim_to_near(layer):
        return remote(
            pool.at[layer, 1, NEAR],
            pool.at[layer, 0, NEAR],
            near_send.at[layer],
            near_recv.at[layer],
            (z, shadow),
        )

    def part_of(layer, part):
        return weights.at[layer, pl.ds(part * PART, PART)]

    def down_copy(step, part):
        ref = part_of(lax.rem(z + step - 1, sections), part)
        at = (step - 1, part)
        return remote(ref, ref, down_send.at[at], down_recv.at[at], (below, p))

    def down_arrival(step, part):
        ref = part_of(lax.rem(z + step, sections), part)
        at = (step - 1, part)
        return remote(ref, ref, down_send.at[at], down_recv.at[at], (below, p))

    def up_copy(step, part):
        ref = part_of(lax.rem(z - step + 1 + sections, sections), part)
        at = (step - 1, part)
        return remote(ref, ref, up_send.at[at], up_recv.at[at], (above, p))

    def up_arrival(step, part):
        ref = part_of(lax.rem(z - step + sections, sections), part)
        at = (step - 1, part)
        return remote(ref, ref, up_send.at[at], up_recv.at[at], (above, p))

    def sends_up(step):
        return (step <= up_steps) & (step <= z + 1) & (z < sections - 1)

    def to_side(layer, part):
        ref = part_of(layer, part)
        return remote(
            ref, ref, side_send.at[layer, part], side_recv.at[layer, part], (z, sibling)
        )

    def relay_down(step):
        @pl.when((core == 1) & (step <= down_steps))
        def _():
            layer = lax.rem(z + step, sections)
            for part in range(PARTS):
                down_arrival(step, part).wait_recv()

                @pl.when(step < down_steps)
                def _():
                    down_copy(step + 1, part).start()

                @pl.when(layer < layers)
                def _():
                    to_side(layer, part).start()

    def relay_up(step):
        @pl.when((core == 1) & (step <= up_steps) & (step <= z))
        def _():
            for part in range(PARTS):
                up_arrival(step, part).wait_recv()

                @pl.when(sends_up(step + 1))
                def _():
                    up_copy(step + 1, part).start()

                to_side(z - step, part).start()

    def have_weight(layer):
        @pl.when((core == 0) & (layer != z))
        def _():
            for part in range(PARTS):
                to_side(layer, part).wait_recv()

    def out_local():
        return pltpu.make_async_copy(pool.at[z + 1, 0, ALL], out_ref.at[0, span], out_send.at[0])

    def out_remote(half):
        return remote(
            pool.at[pair + 1, 0, ALL],
            out_ref.at[0, half],
            out_send.at[1],
            out_recv.at[0],
            (pair, p),
        )

    ordinals = np.arange(sections, dtype=np.float32)
    mixings = np.log(np.float32(lambda_decay) / (ordinals + np.float32(1.0)) + np.float32(1.0))
    for layer in range(sections):
        betas[layer] = jnp.float32(mixings[layer])
    for copy in inputs[:3]:
        copy.wait()
    wanted = jnp.where(span == 0, rows[0:1, :], rows[1:2, :])
    live = lax.broadcasted_iota(jnp.int32, (1, RIM), 1) < count[0, span]
    notes[0, 16:17, :] = jnp.where(live, wanted, -1).astype(jnp.float32)
    inputs[4].wait()
    for block in range(OWN):
        first = sources[span, 3 * block]
        second = sources[span, 3 * block + 1]
        third = sources[span, 3 * block + 2]
        at_before = jnp.where(second == OWN, 1, 0) + jnp.where(third == OWN, 2, 0)
        at_after = jnp.where(second == OWN + 1, 1, 0) + jnp.where(third == OWN + 1, 2, 0)
        at_own = jnp.minimum(3 - at_before - at_after, 2)
        own_tile = first + second + third - (2 * OWN + 1)
        place = pl.ds(block * TILE, TILE)
        at_far = jnp.where(core == 1, at_before, at_after)
        at_near = jnp.where(core == 1, at_after, at_before)
        edge[0, place, 0:RIM] = tiles[3 * block + at_far]
        edge[0, place, RIM : 2 * RIM] = tiles[3 * block + at_near]
        tight[0, place] = tiles[3 * block + at_own]
        for t in range(OWN):
            chosen = jnp.where(own_tile == t, 1.0, 0.0)
            notes[0, 4 * block + t : 4 * block + t + 1, :] = jnp.full((1, TILE), chosen)

    lane = lax.broadcasted_iota(jnp.int32, (RIM, TILE), 1).astype(jnp.float32)

    def picker(unit):
        turned = jnp.broadcast_to(notes[unit, 16:17, :], (RIM, RIM)).T
        return jnp.concatenate(
            [jnp.where(turned == lane + float(t * TILE), 1.0, 0.0) for t in range(OWN)], axis=1
        ).astype(jnp.bfloat16)

    def first_rim(unit):
        pool[0, 1 - unit, NEAR] = dot(picker(unit), pool[0, unit, ALL]).astype(jnp.bfloat16)

    def spread(unit):
        pick = picker(unit)
        for block in range(OWN):
            place = pl.ds(block * TILE, TILE)
            own = tight[unit, place].astype(jnp.float32)
            for t in range(OWN):
                mask = notes[unit, 4 * block + t : 4 * block + t + 1, :]
                wide[unit, place, t * TILE : (t + 1) * TILE] = (own * mask).astype(jnp.bfloat16)
        rim_wide[unit] = dot(pick, wide[unit]).astype(jnp.bfloat16)
        rim_edge[unit] = dot(pick, edge[unit]).astype(jnp.bfloat16)

    def start_rim(unit, layer):
        early[unit] = dot(rim_wide[unit], pool[layer, unit, ALL])

    def finish(aggregate, anchor, layer):
        mixing = betas[layer]
        blended = (1.0 - alpha_mix) * aggregate + alpha_mix * anchor.astype(jnp.float32)
        projected = dot(blended.astype(jnp.bfloat16), weights[layer])
        return jnp.maximum((1.0 - mixing) * blended + mixing * projected, 0.0).astype(jnp.bfloat16)

    def end_rim(unit, layer):
        aggregate = early[unit] + dot(rim_edge[unit], pool[layer, unit, EDGES])
        pool[layer + 1, 1 - unit, NEAR] = finish(aggregate, pool[0, 1 - unit, NEAR], layer)

    def all_rows(unit, layer):
        aggregate = dot(wide[unit], pool[layer, unit, ALL])
        aggregate += dot(edge[unit], pool[layer, unit, EDGES])
        pool[layer + 1, unit, ALL] = finish(aggregate, pool[0, unit, ALL], layer)

    inputs[3].wait()
    first_rim(0)
    spread(0)
    inputs[5].wait()
    pl.semaphore_wait(barrier, len(greeted))
    for copy in (rim_to_sibling(0), rim_to_near(0), rim_to_far(0)):
        copy.start()

    @pl.when(core == 1)
    def _():
        for part in range(PARTS):
            down_copy(1, part).start()

            @pl.when(sends_up(1))
            def _():
                up_copy(1, part).start()

    for item in (0, 2, 3, 1):
        ship(item).start()
    start_rim(0, 0)

    down_first = jnp.minimum(sections + 1 - z, down_steps)
    up_first = jnp.minimum(sections - z, up_steps)

    def relay(step, carry):
        @pl.when(step <= down_first)
        def _():
            relay_down(step)

        @pl.when(step <= up_first)
        def _():
            relay_up(step)

        return carry

    lax.fori_loop(1, down_steps + 1, relay, 0)
    have_weight(0)
    rim_to_sibling(0).wait_recv()
    rim_to_near(0).wait_recv()
    end_rim(0, 0)
    rim_to_sibling(1).start()
    rim_to_near(1).start()

    @pl.when(layers > 2)
    def _():
        rim_to_far(1).start()

    all_rows(0, 0)
    start_rim(0, 1)
    relay_down(down_first + 1)
    have_weight(1)
    rim_to_sibling(1).wait_recv()
    rim_to_near(1).wait_recv()

    @pl.when(layers > 2)
    def _():
        end_rim(0, 1)
        rim_to_sibling(2).start()

        @pl.when(layers > 3)
        def _():
            rim_to_far(2).start()

    all_rows(0, 1)
    relay_down(down_first + 2)
    ship(0).wait_recv()
    ship(2).wait_recv()
    ship(3).wait_recv()
    spread(1)
    ship(1).wait_recv()
    rim_to_far(0).wait_recv()

    @pl.when(layers > 2)
    def _():
        start_rim(0, 2)
        all_rows(1, 0)
        start_rim(1, 1)

    def first_out():
        @pl.when(span == 0)
        def _():
            out_local().start()

        @pl.when(span == 1)
        def _():
            out_remote(span).start()

    def step(i, carry):
        @pl.when(i == layers - 2)
        def _():
            first_out()

        rim_to_far(i).wait_recv()
        end_rim(1, i)
        have_weight(i + 1)
        rim_to_sibling(i + 1).wait_recv()

        @pl.when(i < layers - 2)
        def _():
            end_rim(0, i + 1)
            rim_to_sibling(i + 2).start()

            @pl.when(i < layers - 3)
            def _():
                rim_to_far(i + 2).start()

            relay_down(down_first + 2 + i)
            relay_up(up_first + i)
            all_rows(1, i)
            start_rim(1, i + 1)

        all_rows(0, i + 1)

        @pl.when(i < layers - 2)
        def _():
            start_rim(0, i + 2)

        return carry

    lax.fori_loop(1, layers - 1, step, 0)

    @pl.when(layers == 2)
    def _():
        first_out()

    @pl.when(span == 1)
    def _():
        out_local().start()

    @pl.when(span == 0)
    def _():
        out_remote(span).start()

    for item in range(4):
        ship(item).wait_send()
    for layer in range(2):
        rim_to_near(layer).wait_send()

    def sent(layer, carry):
        rim_to_sibling(layer).wait_send()

        @pl.when(layer < layers - 1)
        def _():
            rim_to_far(layer).wait_send()

        @pl.when((core == 1) & (layer != z))
        def _():
            for part in range(PARTS):
                to_side(layer, part).wait_send()

        return carry

    lax.fori_loop(0, layers, sent, 0)

    @pl.when(core == 1)
    def _():
        for part in range(PARTS):
            for step in range(1, down_steps + 1):
                down_copy(step, part).wait_send()
            for step in range(1, up_steps + 1):

                @pl.when(sends_up(step))
                def _():
                    up_copy(step, part).wait_send()

    out_local().wait()
    out_remote(span).wait_send()
    out_remote(1 - span).wait_recv()


def solution(mesh):
    sections, shards = mesh.shape["section"], mesh.shape["node"]

    def on_device(initial, adjacency, sources, boundary_rows, boundary_count, layer_weights):
        def body(*refs):
            layers_kernel(sections, shards, *refs)

        dma = pltpu.SemaphoreType.DMA
        down_steps = sections // 2
        return pl.pallas_call(
            body,
            out_shape=jax.ShapeDtypeStruct((1, SPANS, ROWS, WIDTH), jnp.bfloat16),
            in_specs=[pl.BlockSpec(memory_space=pltpu.HBM)] * 6,
            out_specs=pl.BlockSpec(memory_space=pltpu.HBM),
            scratch_shapes=[
                pltpu.SMEM((sections,), jnp.float32),
                pltpu.VMEM((OWN * 3, TILE, TILE), jnp.bfloat16),
                pltpu.SMEM((SPANS, OWN * 3), jnp.int32),
                pltpu.VMEM((SPANS, RIM), jnp.int32),
                pltpu.SMEM((1, SPANS), jnp.int32),
                pltpu.VMEM((sections, WIDTH, WIDTH), jnp.bfloat16),
                pltpu.VMEM((sections + 1, 2, POOL, WIDTH), jnp.bfloat16),
                pltpu.VMEM((2, ROWS, ROWS), jnp.bfloat16),
                pltpu.VMEM((2, ROWS, 2 * RIM), jnp.bfloat16),
                pltpu.VMEM((2, ROWS, TILE), jnp.bfloat16),
                pltpu.VMEM((2, NOTES, TILE), jnp.float32),
                pltpu.VMEM((2, RIM, ROWS), jnp.bfloat16),
                pltpu.VMEM((2, RIM, 2 * RIM), jnp.bfloat16),
                pltpu.VMEM((2, RIM, WIDTH), jnp.float32),
                dma((4,)),
                dma((4,)),
                dma((sections, 2)),
                dma((sections, 2)),
                dma((2,)),
                dma((2,)),
                dma((down_steps, PARTS)),
                dma((down_steps, PARTS)),
                dma((down_steps, PARTS)),
                dma((down_steps, PARTS)),
                dma((sections, PARTS)),
                dma((sections, PARTS)),
                dma((2,)),
                dma((1,)),
                dma((6,)),
            ],
            compiler_params=pltpu.CompilerParams(
                collective_id=0, has_side_effects=True, vmem_limit_bytes=60 * 1024 * 1024
            ),
        )(
            initial,
            adjacency,
            sources,
            boundary_rows,
            boundary_count.reshape(1, SPANS),
            layer_weights,
        )

    in_specs = (
        P(None, "node", None),
        P(None, "node", None, None),
        P(None, "node"),
        P(None, "node"),
        P(None, "node"),
        P("section", None, None),
    )
    out_specs = P("section", None, "node", None)
    return jax.shard_map(
        on_device, mesh=mesh, in_specs=in_specs, out_specs=out_specs, check_vma=False
    )
```

```python
import jax
import jax.numpy as jnp
import numpy as np
from jax import lax
from jax.experimental import pallas as pl
from jax.experimental.pallas import tpu as pltpu
from jax.sharding import PartitionSpec as P

MESH = pl.DeviceIdType.MESH

alpha_mix = 0.1
lambda_decay = 0.5

SPANS = 2
ROWS = 512
TILE = 128
WIDTH = 256
RIM = 128
OWN = ROWS // TILE
POOL = ROWS + 2 * RIM
PARTS = 2
PART = WIDTH // PARTS
NOTES = 24

ALL = pl.ds(0, ROWS)
FAR = pl.ds(ROWS, RIM)
NEAR = pl.ds(ROWS + RIM, RIM)
EDGES = pl.ds(ROWS, 2 * RIM)


def dot(a, b):
    return jnp.dot(a, b, preferred_element_type=jnp.float32)


def layers_kernel(
    sections,
    shards,
    initial_ref,
    adjacency_ref,
    sources_ref,
    rows_ref,
    count_ref,
    weight_ref,
    out_ref,
    betas,
    tiles,
    sources,
    rows,
    count,
    weights,
    pool,
    wide,
    edge,
    tight,
    notes,
    rim_wide,
    rim_edge,
    early,
    ship_send,
    ship_recv,
    rim_send,
    rim_recv,
    near_send,
    near_recv,
    server_send,
    down_send,
    down_recv,
    up_send,
    up_recv,
    side_send,
    side_recv,
    out_send,
    out_recv,
    in_sem,
):
    z = lax.axis_index("section")
    p = lax.axis_index("node")
    span = lax.rem(z, 2)
    core = lax.rem(p, 2)
    shadow = lax.rem(p - 1 + 2 * core + shards, shards)
    sibling = p + 1 - 2 * core
    far_to = lax.rem(p + 2 - 4 * core + shards, shards)
    far_from = lax.rem(p - 2 + 4 * core + shards, shards)
    below, above = lax.rem(z + sections - 1, sections), lax.rem(z + 1, sections)
    server = z == sections - 2
    layers = jnp.where(server, sections, jnp.maximum(z + 1, 2))
    middle = sections // 2
    up_steps = middle - 1

    barrier = pltpu.get_barrier_semaphore()
    greeted = [(z, node) for node in (sibling, far_to, far_from, shadow)]
    greeted += [(below, p), (above, p)]
    for device in greeted:
        pl.semaphore_signal(barrier, inc=1, device_id=device, device_id_type=MESH)

    @pl.when((core == 1) & server)
    def _():
        pl.semaphore_signal(barrier, inc=1, device_id=(0, p), device_id_type=MESH)

    greetings = len(greeted) + jnp.where((core == 1) & (z == 0), 1, 0)

    inputs = [
        pltpu.make_async_copy(src, dst, in_sem.at[index])
        for index, (src, dst) in enumerate(
            (
                (sources_ref, sources),
                (count_ref, count),
                (rows_ref, rows),
                (initial_ref.at[span], pool.at[0, 0, ALL]),
                (adjacency_ref.at[span], tiles),
                (weight_ref.at[0], weights.at[z]),
            )
        )
    ]
    for copy in inputs:
        copy.start()

    def remote(src, dst, send, recv, device):
        return pltpu.make_async_remote_copy(
            src_ref=src,
            dst_ref=dst,
            send_sem=send,
            recv_sem=recv,
            device_id=device,
            device_id_type=MESH,
        )

    def ship(item):
        refs = (
            (notes.at[0], notes.at[1]),
            (pool.at[0, 0, ALL], pool.at[0, 1, ALL]),
            (tight.at[0], tight.at[1]),
            (edge.at[0], edge.at[1]),
        )[item]
        return remote(*refs, ship_send.at[item], ship_recv.at[item], (z, shadow))

    def rim_to_sibling(layer):
        return remote(
            pool.at[layer, 1, NEAR],
            pool.at[layer, 0, FAR],
            rim_send.at[layer, 0],
            rim_recv.at[layer, 0],
            (z, sibling),
        )

    def rim_to_far(layer):
        return remote(
            pool.at[layer, 1, NEAR],
            pool.at[layer, 1, FAR],
            rim_send.at[layer, 1],
            rim_recv.at[layer, 1],
            (z, far_to),
        )

    def rim_to_near(layer):
        return remote(
            pool.at[layer, 1, NEAR],
            pool.at[layer, 0, NEAR],
            near_send.at[layer],
            near_recv.at[layer],
            (z, shadow),
        )

    def part_of(layer, part):
        return weights.at[layer, pl.ds(part * PART, PART)]

    def to_below(layer, part):
        ref = part_of(layer, part)
        return remote(
            ref, ref, down_send.at[layer, part], down_recv.at[layer, part], (below, p)
        )

    def to_server(layer, part):
        ref = part_of(layer, part)
        there = (sections - 2, p)
        return remote(ref, ref, server_send.at[layer, part], down_recv.at[layer, part], there)

    def takes_down(layer):
        lower = (z < middle) & (layer > z) & (layer < middle)
        return (core == 1) & (lower | ((z >= middle) & (layer <= z - middle)))

    def sends_below(layer):
        lower = (z < middle) & (layer >= z) & (layer < middle)
        upper = (z > middle) & (z < sections - 1) & (layer < z - middle)
        return (core == 1) & (lower | upper)

    def sends_server(layer):
        return (core == 1) & (z == 0) & (layer < middle - 1)

    def send_down(layer, part):
        @pl.when(sends_below(layer))
        def _():
            to_below(layer, part).start()

        @pl.when(sends_server(layer))
        def _():
            to_server(layer, part).start()

    def up_copy(step, part):
        ref = part_of(lax.rem(z - step + 1 + sections, sections), part)
        at = (step - 1, part)
        return remote(ref, ref, up_send.at[at], up_recv.at[at], (above, p))

    def up_arrival(step, part):
        ref = part_of(lax.rem(z - step + sections, sections), part)
        at = (step - 1, part)
        return remote(ref, ref, up_send.at[at], up_recv.at[at], (above, p))

    def sends_up(step):
        return (step <= up_steps) & (step <= z + 1) & (z < sections - 1)

    def to_side(layer, part):
        ref = part_of(layer, part)
        return remote(
            ref, ref, side_send.at[layer, part], side_recv.at[layer, part], (z, sibling)
        )

    def relay_down(layer):
        @pl.when(takes_down(layer))
        def _():
            for part in range(PARTS):
                to_below(layer, part).wait_recv()
                send_down(layer, part)

                @pl.when(layer < layers)
                def _():
                    to_side(layer, part).start()

    def take_last():
        @pl.when((core == 1) & server)
        def _():
            for part in range(PARTS):
                to_below(z + 1, part).wait_recv()
                to_side(z + 1, part).start()

    def relay_up(step):
        @pl.when((core == 1) & (step <= up_steps) & (step <= z))
        def _():
            for part in range(PARTS):
                up_arrival(step, part).wait_recv()

                @pl.when(sends_up(step + 1))
                def _():
                    up_copy(step + 1, part).start()

                to_side(z - step, part).start()

    def have_weight(layer):
        @pl.when((core == 0) & (layer != z))
        def _():
            for part in range(PARTS):
                to_side(layer, part).wait_recv()

    def out_local():
        return pltpu.make_async_copy(pool.at[z + 1, 0, ALL], out_ref.at[0, span], out_send.at[0])

    def out_below(half):
        return remote(
            pool.at[z, 0, ALL], out_ref.at[0, half], out_send.at[1], out_recv.at[0], (below, p)
        )

    def out_above():
        return remote(
            pool.at[z + 2, 0, ALL], out_ref.at[0, span], out_send.at[2], out_recv.at[0], (above, p)
        )

    ordinals = np.arange(sections, dtype=np.float32)
    mixings = np.log(np.float32(lambda_decay) / (ordinals + np.float32(1.0)) + np.float32(1.0))
    for layer in range(sections):
        betas[layer] = jnp.float32(mixings[layer])
    for copy in inputs[:3]:
        copy.wait()
    wanted = jnp.where(span == 0, rows[0:1, :], rows[1:2, :])
    live = lax.broadcasted_iota(jnp.int32, (1, RIM), 1) < count[0, span]
    notes[0, 16:17, :] = jnp.where(live, wanted, -1).astype(jnp.float32)
    inputs[4].wait()
    for block in range(OWN):
        first = sources[span, 3 * block]
        second = sources[span, 3 * block + 1]
        third = sources[span, 3 * block + 2]
        at_before = jnp.where(second == OWN, 1, 0) + jnp.where(third == OWN, 2, 0)
        at_after = jnp.where(second == OWN + 1, 1, 0) + jnp.where(third == OWN + 1, 2, 0)
        at_own = jnp.minimum(3 - at_before - at_after, 2)
        own_tile = first + second + third - (2 * OWN + 1)
        place = pl.ds(block * TILE, TILE)
        at_far = jnp.where(core == 1, at_before, at_after)
        at_near = jnp.where(core == 1, at_after, at_before)
        edge[0, place, 0:RIM] = tiles[3 * block + at_far]
        edge[0, place, RIM : 2 * RIM] = tiles[3 * block + at_near]
        tight[0, place] = tiles[3 * block + at_own]
        for t in range(OWN):
            chosen = jnp.where(own_tile == t, 1.0, 0.0)
            notes[0, 4 * block + t : 4 * block + t + 1, :] = jnp.full((1, TILE), chosen)

    lane = lax.broadcasted_iota(jnp.int32, (RIM, TILE), 1).astype(jnp.float32)

    def picker(unit):
        turned = jnp.broadcast_to(notes[unit, 16:17, :], (RIM, RIM)).T
        return jnp.concatenate(
            [jnp.where(turned == lane + float(t * TILE), 1.0, 0.0) for t in range(OWN)], axis=1
        ).astype(jnp.bfloat16)

    def first_rim(unit):
        pool[0, 1 - unit, NEAR] = dot(picker(unit), pool[0, unit, ALL]).astype(jnp.bfloat16)

    def spread(unit):
        pick = picker(unit)
        for block in range(OWN):
            place = pl.ds(block * TILE, TILE)
            own = tight[unit, place].astype(jnp.float32)
            for t in range(OWN):
                mask = notes[unit, 4 * block + t : 4 * block + t + 1, :]
                wide[unit, place, t * TILE : (t + 1) * TILE] = (own * mask).astype(jnp.bfloat16)
        rim_wide[unit] = dot(pick, wide[unit]).astype(jnp.bfloat16)
        rim_edge[unit] = dot(pick, edge[unit]).astype(jnp.bfloat16)

    def start_rim(unit, layer):
        early[unit] = dot(rim_wide[unit], pool[layer, unit, ALL])

    def finish(aggregate, anchor, layer):
        mixing = betas[layer]
        blended = (1.0 - alpha_mix) * aggregate + alpha_mix * anchor.astype(jnp.float32)
        projected = dot(blended.astype(jnp.bfloat16), weights[layer])
        return jnp.maximum((1.0 - mixing) * blended + mixing * projected, 0.0).astype(jnp.bfloat16)

    def end_rim(unit, layer):
        aggregate = early[unit] + dot(rim_edge[unit], pool[layer, unit, EDGES])
        pool[layer + 1, 1 - unit, NEAR] = finish(aggregate, pool[0, 1 - unit, NEAR], layer)

    def all_rows(unit, layer):
        aggregate = dot(wide[unit], pool[layer, unit, ALL])
        aggregate += dot(edge[unit], pool[layer, unit, EDGES])
        pool[layer + 1, unit, ALL] = finish(aggregate, pool[0, unit, ALL], layer)

    inputs[3].wait()
    first_rim(0)
    spread(0)
    inputs[5].wait()
    pl.semaphore_wait(barrier, greetings)
    for copy in (rim_to_sibling(0), rim_to_near(0), rim_to_far(0)):
        copy.start()

    @pl.when(core == 1)
    def _():
        for part in range(PARTS):
            send_down(z, part)

            @pl.when(z == sections - 1)
            def _():
                to_below(z, part).start()

            @pl.when(sends_up(1))
            def _():
                up_copy(1, part).start()

    for item in (0, 2, 3, 1):
        ship(item).start()
    start_rim(0, 0)

    def relay_down_upper(layer):
        @pl.when(z >= middle)
        def _():
            relay_down(layer)

    up_first = jnp.minimum(sections - z, up_steps)

    def relay(step, carry):
        @pl.when(z < middle)
        def _():
            relay_down(z + step)

        @pl.when(step <= up_first)
        def _():
            relay_up(step)

        return carry

    lax.fori_loop(1, middle, relay, 0)
    relay_down_upper(0)
    have_weight(0)
    rim_to_sibling(0).wait_recv()
    rim_to_near(0).wait_recv()
    end_rim(0, 0)
    rim_to_sibling(1).start()
    rim_to_near(1).start()

    @pl.when(layers > 2)
    def _():
        rim_to_far(1).start()

    all_rows(0, 0)
    start_rim(0, 1)
    relay_down_upper(1)
    take_last()
    have_weight(1)
    rim_to_sibling(1).wait_recv()
    rim_to_near(1).wait_recv()

    @pl.when(layers > 2)
    def _():
        end_rim(0, 1)
        rim_to_sibling(2).start()

        @pl.when(layers > 3)
        def _():
            rim_to_far(2).start()

    all_rows(0, 1)
    relay_down_upper(2)
    ship(0).wait_recv()
    ship(2).wait_recv()
    ship(3).wait_recv()
    spread(1)
    ship(1).wait_recv()
    rim_to_far(0).wait_recv()

    @pl.when(layers > 2)
    def _():
        start_rim(0, 2)
        all_rows(1, 0)
        start_rim(1, 1)

    def step(i, carry):
        @pl.when(i == z - 1)
        def _():
            out_below(span).start()

        @pl.when(i == z)
        def _():
            out_local().start()

        rim_to_far(i).wait_recv()
        end_rim(1, i)
        have_weight(i + 1)
        rim_to_sibling(i + 1).wait_recv()

        @pl.when(i < layers - 2)
        def _():
            end_rim(0, i + 1)

            @pl.when(i < layers - 3)
            def _():
                rim_to_far(i + 2).start()

            rim_to_sibling(i + 2).start()

            relay_up(up_first + i)
            all_rows(1, i)
            start_rim(1, i + 1)
            relay_down_upper(i + 2)

        all_rows(0, i + 1)

        @pl.when(i < layers - 2)
        def _():
            start_rim(0, i + 2)

        return carry

    lax.fori_loop(1, layers - 1, step, 0)

    @pl.when(z == 1)
    def _():
        out_below(span).start()

    @pl.when(server)
    def _():
        out_above().start()

    @pl.when(jnp.logical_not(server))
    def _():
        out_local().start()

    for item in range(4):
        ship(item).wait_send()
    for layer in range(2):
        rim_to_near(layer).wait_send()

    def sent(layer, carry):
        rim_to_sibling(layer).wait_send()

        @pl.when(layer < layers - 1)
        def _():
            rim_to_far(layer).wait_send()

        @pl.when((core == 1) & (layer != z))
        def _():
            for part in range(PARTS):
                to_side(layer, part).wait_send()

        return carry

    lax.fori_loop(0, layers, sent, 0)

    @pl.when(core == 1)
    def _():
        for part in range(PARTS):
            for layer in range(middle):

                @pl.when(sends_below(layer))
                def _():
                    to_below(layer, part).wait_send()

                @pl.when(sends_server(layer))
                def _():
                    to_server(layer, part).wait_send()

            @pl.when(z == sections - 1)
            def _():
                to_below(z, part).wait_send()

            for step in range(1, up_steps + 1):

                @pl.when(sends_up(step))
                def _():
                    up_copy(step, part).wait_send()

    out_local().wait()

    @pl.when(z > 0)
    def _():
        out_below(span).wait_send()

    @pl.when(server)
    def _():
        out_above().wait_send()

    out_below(1 - span).wait_recv()


def solution(mesh):
    sections, shards = mesh.shape["section"], mesh.shape["node"]

    def on_device(initial, adjacency, sources, boundary_rows, boundary_count, layer_weights):
        def body(*refs):
            layers_kernel(sections, shards, *refs)

        dma = pltpu.SemaphoreType.DMA
        middle = sections // 2
        return pl.pallas_call(
            body,
            out_shape=jax.ShapeDtypeStruct((1, SPANS, ROWS, WIDTH), jnp.bfloat16),
            in_specs=[pl.BlockSpec(memory_space=pltpu.HBM)] * 6,
            out_specs=pl.BlockSpec(memory_space=pltpu.HBM),
            scratch_shapes=[
                pltpu.SMEM((sections,), jnp.float32),
                pltpu.VMEM((OWN * 3, TILE, TILE), jnp.bfloat16),
                pltpu.SMEM((SPANS, OWN * 3), jnp.int32),
                pltpu.VMEM((SPANS, RIM), jnp.int32),
                pltpu.SMEM((1, SPANS), jnp.int32),
                pltpu.VMEM((sections, WIDTH, WIDTH), jnp.bfloat16),
                pltpu.VMEM((sections + 1, 2, POOL, WIDTH), jnp.bfloat16),
                pltpu.VMEM((2, ROWS, ROWS), jnp.bfloat16),
                pltpu.VMEM((2, ROWS, 2 * RIM), jnp.bfloat16),
                pltpu.VMEM((2, ROWS, TILE), jnp.bfloat16),
                pltpu.VMEM((2, NOTES, TILE), jnp.float32),
                pltpu.VMEM((2, RIM, ROWS), jnp.bfloat16),
                pltpu.VMEM((2, RIM, 2 * RIM), jnp.bfloat16),
                pltpu.VMEM((2, RIM, WIDTH), jnp.float32),
                dma((4,)),
                dma((4,)),
                dma((sections, 2)),
                dma((sections, 2)),
                dma((2,)),
                dma((2,)),
                dma((middle, PARTS)),
                dma((sections, PARTS)),
                dma((sections, PARTS)),
                dma((middle, PARTS)),
                dma((middle, PARTS)),
                dma((sections, PARTS)),
                dma((sections, PARTS)),
                dma((3,)),
                dma((1,)),
                dma((6,)),
            ],
            compiler_params=pltpu.CompilerParams(
                collective_id=0, has_side_effects=True, vmem_limit_bytes=60 * 1024 * 1024
            ),
        )(
            initial,
            adjacency,
            sources,
            boundary_rows,
            boundary_count.reshape(1, SPANS),
            layer_weights,
        )

    in_specs = (
        P(None, "node", None),
        P(None, "node", None, None),
        P(None, "node"),
        P(None, "node"),
        P(None, "node"),
        P("section", None, None),
    )
    out_specs = P("section", None, "node", None)
    return jax.shard_map(
        on_device, mesh=mesh, in_specs=in_specs, out_specs=out_specs, check_vma=False
    )
```

```python
import jax
import jax.numpy as jnp
import numpy as np
from jax import lax
from jax.experimental import pallas as pl
from jax.experimental.pallas import tpu as pltpu
from jax.sharding import PartitionSpec as P

MESH = pl.DeviceIdType.MESH

alpha_mix = 0.1
lambda_decay = 0.5

SPANS = 2
ROWS = 512
TILE = 128
WIDTH = 256
RIM = 128
OWN = ROWS // TILE
POOL = ROWS + 2 * RIM
PARTS = 2
PART = WIDTH // PARTS
NOTES = 24

ALL = pl.ds(0, ROWS)
FAR = pl.ds(ROWS, RIM)
NEAR = pl.ds(ROWS + RIM, RIM)
EDGES = pl.ds(ROWS, 2 * RIM)


def dot(a, b):
    return jnp.dot(a, b, preferred_element_type=jnp.float32)


def layers_kernel(
    sections,
    shards,
    initial_ref,
    adjacency_ref,
    sources_ref,
    rows_ref,
    count_ref,
    weight_ref,
    out_ref,
    betas,
    tiles,
    sources,
    rows,
    count,
    weights,
    pool,
    wide,
    edge,
    tight,
    notes,
    rim_wide,
    rim_edge,
    early,
    ship_send,
    ship_recv,
    rim_send,
    rim_recv,
    near_send,
    near_recv,
    server_send,
    down_send,
    down_recv,
    up_send,
    up_recv,
    side_send,
    side_recv,
    out_send,
    out_recv,
    in_sem,
):
    z = lax.axis_index("section")
    p = lax.axis_index("node")
    span = lax.rem(z, 2)
    core = lax.rem(p, 2)
    shadow = lax.rem(p - 1 + 2 * core + shards, shards)
    sibling = p + 1 - 2 * core
    far_to = lax.rem(p + 2 - 4 * core + shards, shards)
    far_from = lax.rem(p - 2 + 4 * core + shards, shards)
    below, above = lax.rem(z + sections - 1, sections), lax.rem(z + 1, sections)
    server = z == sections - 2
    layers = jnp.where(server, sections, jnp.maximum(z + 1, 2))
    middle = sections // 2
    up_steps = middle - 1

    barrier = pltpu.get_barrier_semaphore()
    greeted = [(z, node) for node in (sibling, far_to, far_from, shadow)]
    greeted += [(below, p), (above, p)]
    for device in greeted:
        pl.semaphore_signal(barrier, inc=1, device_id=device, device_id_type=MESH)

    @pl.when((core == 1) & server)
    def _():
        pl.semaphore_signal(barrier, inc=1, device_id=(0, p), device_id_type=MESH)

    greetings = len(greeted) + jnp.where((core == 1) & (z == 0), 1, 0)

    inputs = [
        pltpu.make_async_copy(src, dst, in_sem.at[index])
        for index, (src, dst) in enumerate(
            (
                (sources_ref, sources),
                (count_ref, count),
                (rows_ref, rows),
                (initial_ref.at[span], pool.at[0, 0, ALL]),
                (adjacency_ref.at[span], tiles),
                (weight_ref.at[0], weights.at[z]),
            )
        )
    ]
    for copy in inputs:
        copy.start()

    def remote(src, dst, send, recv, device):
        return pltpu.make_async_remote_copy(
            src_ref=src,
            dst_ref=dst,
            send_sem=send,
            recv_sem=recv,
            device_id=device,
            device_id_type=MESH,
        )

    def ship(item):
        refs = (
            (notes.at[0], notes.at[1]),
            (pool.at[0, 0, ALL], pool.at[0, 1, ALL]),
            (tight.at[0], tight.at[1]),
            (edge.at[0], edge.at[1]),
        )[item]
        return remote(*refs, ship_send.at[item], ship_recv.at[item], (z, shadow))

    def rim_to_sibling(layer):
        return remote(
            pool.at[layer, 1, NEAR],
            pool.at[layer, 0, FAR],
            rim_send.at[layer, 0],
            rim_recv.at[layer, 0],
            (z, sibling),
        )

    def rim_to_far(layer):
        return remote(
            pool.at[layer, 1, NEAR],
            pool.at[layer, 1, FAR],
            rim_send.at[layer, 1],
            rim_recv.at[layer, 1],
            (z, far_to),
        )

    def rim_to_near(layer):
        return remote(
            pool.at[layer, 1, NEAR],
            pool.at[layer, 0, NEAR],
            near_send.at[layer],
            near_recv.at[layer],
            (z, shadow),
        )

    def part_of(layer, part):
        return weights.at[layer, pl.ds(part * PART, PART)]

    def to_below(layer, part):
        ref = part_of(layer, part)
        return remote(
            ref, ref, down_send.at[layer, part], down_recv.at[layer, part], (below, p)
        )

    def to_server(layer, part):
        ref = part_of(layer, part)
        there = (sections - 2, p)
        return remote(ref, ref, server_send.at[layer, part], down_recv.at[layer, part], there)

    def takes_down(layer):
        lower = (z < middle) & (layer > z) & (layer < middle)
        return (core == 1) & (lower | ((z >= middle) & (layer <= z - middle)))

    def sends_below(layer):
        lower = (z < middle) & (layer >= z) & (layer < middle)
        upper = (z > middle) & (z < sections - 1) & (layer < z - middle)
        return (core == 1) & (lower | upper)

    def sends_server(layer):
        return (core == 1) & (z == 0) & (layer < middle - 1)

    def send_down(layer, part):
        @pl.when(sends_below(layer))
        def _():
            to_below(layer, part).start()

        @pl.when(sends_server(layer))
        def _():
            to_server(layer, part).start()

    def up_copy(step, part):
        ref = part_of(lax.rem(z - step + 1 + sections, sections), part)
        at = (step - 1, part)
        return remote(ref, ref, up_send.at[at], up_recv.at[at], (above, p))

    def up_arrival(step, part):
        ref = part_of(lax.rem(z - step + sections, sections), part)
        at = (step - 1, part)
        return remote(ref, ref, up_send.at[at], up_recv.at[at], (above, p))

    def sends_up(step):
        return (step <= up_steps) & (step <= z + 1) & (z < sections - 1)

    def to_side(layer, part):
        ref = part_of(layer, part)
        return remote(
            ref, ref, side_send.at[layer, part], side_recv.at[layer, part], (z, sibling)
        )

    def relay_down(layer):
        @pl.when(takes_down(layer))
        def _():
            for part in range(PARTS):
                to_below(layer, part).wait_recv()
                send_down(layer, part)

                @pl.when(layer < layers)
                def _():
                    to_side(layer, part).start()

    def take_last():
        @pl.when((core == 1) & server)
        def _():
            for part in range(PARTS):
                to_below(z + 1, part).wait_recv()
                to_side(z + 1, part).start()

    def relay_up(step):
        @pl.when((core == 1) & (step <= up_steps) & (step <= z))
        def _():
            for part in range(PARTS):
                up_arrival(step, part).wait_recv()

                @pl.when(sends_up(step + 1))
                def _():
                    up_copy(step + 1, part).start()

                to_side(z - step, part).start()

    def have_weight(layer):
        @pl.when((core == 0) & (layer != z))
        def _():
            for part in range(PARTS):
                to_side(layer, part).wait_recv()

    def out_local():
        return pltpu.make_async_copy(pool.at[z + 1, 0, ALL], out_ref.at[0, span], out_send.at[0])

    def out_below(half):
        return remote(
            pool.at[z, 0, ALL], out_ref.at[0, half], out_send.at[1], out_recv.at[0], (below, p)
        )

    def out_above():
        return remote(
            pool.at[z + 2, 0, ALL], out_ref.at[0, span], out_send.at[2], out_recv.at[0], (above, p)
        )

    ordinals = np.arange(sections, dtype=np.float32)
    mixings = np.log(np.float32(lambda_decay) / (ordinals + np.float32(1.0)) + np.float32(1.0))
    for layer in range(sections):
        betas[layer] = jnp.float32(mixings[layer])
    for copy in inputs[:3]:
        copy.wait()
    wanted = jnp.where(span == 0, rows[0:1, :], rows[1:2, :])
    live = lax.broadcasted_iota(jnp.int32, (1, RIM), 1) < count[0, span]
    notes[0, 16:17, :] = jnp.where(live, wanted, -1).astype(jnp.float32)
    inputs[4].wait()
    for block in range(OWN):
        first = sources[span, 3 * block]
        second = sources[span, 3 * block + 1]
        third = sources[span, 3 * block + 2]
        at_before = jnp.where(second == OWN, 1, 0) + jnp.where(third == OWN, 2, 0)
        at_after = jnp.where(second == OWN + 1, 1, 0) + jnp.where(third == OWN + 1, 2, 0)
        at_own = jnp.minimum(3 - at_before - at_after, 2)
        own_tile = first + second + third - (2 * OWN + 1)
        place = pl.ds(block * TILE, TILE)
        at_far = jnp.where(core == 1, at_before, at_after)
        at_near = jnp.where(core == 1, at_after, at_before)
        edge[0, place, 0:RIM] = tiles[3 * block + at_far]
        edge[0, place, RIM : 2 * RIM] = tiles[3 * block + at_near]
        tight[0, place] = tiles[3 * block + at_own]
        for t in range(OWN):
            chosen = jnp.where(own_tile == t, 1.0, 0.0)
            notes[0, 4 * block + t : 4 * block + t + 1, :] = jnp.full((1, TILE), chosen)

    lane = lax.broadcasted_iota(jnp.int32, (RIM, TILE), 1).astype(jnp.float32)

    def picker(unit):
        turned = jnp.broadcast_to(notes[unit, 16:17, :], (RIM, RIM)).T
        return jnp.concatenate(
            [jnp.where(turned == lane + float(t * TILE), 1.0, 0.0) for t in range(OWN)], axis=1
        ).astype(jnp.bfloat16)

    def first_rim(unit):
        pool[0, 1 - unit, NEAR] = dot(picker(unit), pool[0, unit, ALL]).astype(jnp.bfloat16)

    def spread(unit):
        pick = picker(unit)
        for block in range(OWN):
            place = pl.ds(block * TILE, TILE)
            own = tight[unit, place].astype(jnp.float32)
            for t in range(OWN):
                mask = notes[unit, 4 * block + t : 4 * block + t + 1, :]
                wide[unit, place, t * TILE : (t + 1) * TILE] = (own * mask).astype(jnp.bfloat16)
        rim_wide[unit] = dot(pick, wide[unit]).astype(jnp.bfloat16)
        rim_edge[unit] = dot(pick, edge[unit]).astype(jnp.bfloat16)

    def start_rim(unit, layer):
        early[unit] = dot(rim_wide[unit], pool[layer, unit, ALL])

    def blend(aggregate, anchor):
        return (1.0 - alpha_mix) * aggregate + alpha_mix * anchor.astype(jnp.float32)

    def finish(blended, blended_b, layer):
        mixing = betas[layer]
        projected = dot(blended_b, weights[layer])
        return jnp.maximum((1.0 - mixing) * blended + mixing * projected, 0.0).astype(jnp.bfloat16)

    def rim_blend(unit, layer):
        aggregate = early[unit] + dot(rim_edge[unit], pool[layer, unit, EDGES])
        return blend(aggregate, pool[0, 1 - unit, NEAR])

    def end_rim(unit, layer):
        blended = rim_blend(unit, layer)
        rim = finish(blended, blended.astype(jnp.bfloat16), layer)
        pool[layer + 1, 1 - unit, NEAR] = rim

    def end_own_rim(layer):
        end_rim(0, layer)
        rim_to_far(layer + 1).start()
        rim_to_sibling(layer + 1).start()

    def all_rows(unit, layer):
        aggregate = dot(wide[unit], pool[layer, unit, ALL])
        aggregate += dot(edge[unit], pool[layer, unit, EDGES])
        blended = blend(aggregate, pool[0, unit, ALL])
        rows_b = blended.astype(jnp.bfloat16)
        pool[layer + 1, unit, ALL] = finish(blended, rows_b, layer)

    inputs[3].wait()
    first_rim(0)
    spread(0)
    inputs[5].wait()
    pl.semaphore_wait(barrier, greetings)
    for copy in (rim_to_far(0), rim_to_near(0), rim_to_sibling(0)):
        copy.start()

    @pl.when(core == 1)
    def _():
        for part in range(PARTS):
            send_down(z, part)

            @pl.when(z == sections - 1)
            def _():
                to_below(z, part).start()

            @pl.when(sends_up(1))
            def _():
                up_copy(1, part).start()

    for item in (0, 2, 3, 1):
        ship(item).start()
    start_rim(0, 0)

    def relay_down_upper(layer):
        @pl.when(z >= middle)
        def _():
            relay_down(layer)

    up_first = jnp.minimum(sections - z, up_steps)

    def relay(step, carry):
        @pl.when(z < middle)
        def _():
            relay_down(z + step)

        @pl.when(step <= up_first)
        def _():
            relay_up(step)

        return carry

    lax.fori_loop(1, middle, relay, 0)
    relay_down_upper(0)
    have_weight(0)
    rim_to_sibling(0).wait_recv()
    rim_to_near(0).wait_recv()
    end_own_rim(0)
    rim_to_near(1).start()
    all_rows(0, 0)
    start_rim(0, 1)
    relay_down_upper(1)
    take_last()
    have_weight(1)
    rim_to_sibling(1).wait_recv()
    rim_to_near(1).wait_recv()

    @pl.when(layers > 2)
    def _():
        end_own_rim(1)

    all_rows(0, 1)
    relay_down_upper(2)
    ship(0).wait_recv()
    ship(2).wait_recv()
    ship(3).wait_recv()
    spread(1)
    ship(1).wait_recv()
    rim_to_far(0).wait_recv()

    @pl.when(layers > 2)
    def _():
        start_rim(0, 2)
        all_rows(1, 0)
        start_rim(1, 1)

    def step(i, carry):
        @pl.when(i == z - 1)
        def _():
            out_below(span).start()

        @pl.when(i == z)
        def _():
            out_local().start()

        rim_to_far(i).wait_recv()
        end_rim(1, i)
        have_weight(i + 1)
        rim_to_sibling(i + 1).wait_recv()

        @pl.when(i < layers - 2)
        def _():
            end_own_rim(i + 1)

            relay_up(up_first + i)
            all_rows(1, i)
            start_rim(1, i + 1)
            relay_down_upper(i + 2)

        all_rows(0, i + 1)

        @pl.when(i < layers - 2)
        def _():
            start_rim(0, i + 2)

        return carry

    lax.fori_loop(1, layers - 1, step, 0)

    @pl.when(z == 1)
    def _():
        out_below(span).start()

    @pl.when(server)
    def _():
        out_above().start()

    @pl.when(jnp.logical_not(server))
    def _():
        out_local().start()

    for item in range(4):
        ship(item).wait_send()
    for layer in range(2):
        rim_to_near(layer).wait_send()

    def sent(layer, carry):
        rim_to_sibling(layer).wait_send()
        rim_to_far(layer).wait_send()

        @pl.when((core == 1) & (layer != z))
        def _():
            for part in range(PARTS):
                to_side(layer, part).wait_send()

        return carry

    lax.fori_loop(0, layers, sent, 0)
    rim_to_far(layers - 1).wait_recv()

    @pl.when(core == 1)
    def _():
        for part in range(PARTS):
            for layer in range(middle):

                @pl.when(sends_below(layer))
                def _():
                    to_below(layer, part).wait_send()

                @pl.when(sends_server(layer))
                def _():
                    to_server(layer, part).wait_send()

            @pl.when(z == sections - 1)
            def _():
                to_below(z, part).wait_send()

            for step in range(1, up_steps + 1):

                @pl.when(sends_up(step))
                def _():
                    up_copy(step, part).wait_send()

    out_local().wait()

    @pl.when(z > 0)
    def _():
        out_below(span).wait_send()

    @pl.when(server)
    def _():
        out_above().wait_send()

    out_below(1 - span).wait_recv()


def solution(mesh):
    sections, shards = mesh.shape["section"], mesh.shape["node"]

    def on_device(initial, adjacency, sources, boundary_rows, boundary_count, layer_weights):
        def body(*refs):
            layers_kernel(sections, shards, *refs)

        dma = pltpu.SemaphoreType.DMA
        middle = sections // 2
        return pl.pallas_call(
            body,
            out_shape=jax.ShapeDtypeStruct((1, SPANS, ROWS, WIDTH), jnp.bfloat16),
            in_specs=[pl.BlockSpec(memory_space=pltpu.HBM)] * 6,
            out_specs=pl.BlockSpec(memory_space=pltpu.HBM),
            scratch_shapes=[
                pltpu.SMEM((sections,), jnp.float32),
                pltpu.VMEM((OWN * 3, TILE, TILE), jnp.bfloat16),
                pltpu.SMEM((SPANS, OWN * 3), jnp.int32),
                pltpu.VMEM((SPANS, RIM), jnp.int32),
                pltpu.SMEM((1, SPANS), jnp.int32),
                pltpu.VMEM((sections, WIDTH, WIDTH), jnp.bfloat16),
                pltpu.VMEM((sections + 1, 2, POOL, WIDTH), jnp.bfloat16),
                pltpu.VMEM((2, ROWS, ROWS), jnp.bfloat16),
                pltpu.VMEM((2, ROWS, 2 * RIM), jnp.bfloat16),
                pltpu.VMEM((2, ROWS, TILE), jnp.bfloat16),
                pltpu.VMEM((2, NOTES, TILE), jnp.float32),
                pltpu.VMEM((2, RIM, ROWS), jnp.bfloat16),
                pltpu.VMEM((2, RIM, 2 * RIM), jnp.bfloat16),
                pltpu.VMEM((2, RIM, WIDTH), jnp.float32),
                dma((4,)),
                dma((4,)),
                dma((sections, 2)),
                dma((sections, 2)),
                dma((2,)),
                dma((2,)),
                dma((middle, PARTS)),
                dma((sections, PARTS)),
                dma((sections, PARTS)),
                dma((middle, PARTS)),
                dma((middle, PARTS)),
                dma((sections, PARTS)),
                dma((sections, PARTS)),
                dma((3,)),
                dma((1,)),
                dma((6,)),
            ],
            compiler_params=pltpu.CompilerParams(
                collective_id=0, has_side_effects=True, vmem_limit_bytes=60 * 1024 * 1024
            ),
        )(
            initial,
            adjacency,
            sources,
            boundary_rows,
            boundary_count.reshape(1, SPANS),
            layer_weights,
        )

    in_specs = (
        P(None, "node", None),
        P(None, "node", None, None),
        P(None, "node"),
        P(None, "node"),
        P(None, "node"),
        P("section", None, None),
    )
    out_specs = P("section", None, "node", None)
    return jax.shard_map(
        on_device, mesh=mesh, in_specs=in_specs, out_specs=out_specs, check_vma=False
    )
```

```python
import jax
import jax.numpy as jnp
import numpy as np
from jax import lax
from jax.experimental import pallas as pl
from jax.experimental.pallas import tpu as pltpu
from jax.sharding import PartitionSpec as P

MESH = pl.DeviceIdType.MESH

alpha_mix = 0.1
lambda_decay = 0.5

SPANS = 2
ROWS = 512
TILE = 128
WIDTH = 256
RIM = 128
OWN = ROWS // TILE
POOL = ROWS + 2 * RIM
PARTS = 2
PART = WIDTH // PARTS
NOTES = 24

ALL = pl.ds(0, ROWS)
FAR = pl.ds(ROWS, RIM)
NEAR = pl.ds(ROWS + RIM, RIM)
EDGES = pl.ds(ROWS, 2 * RIM)


def dot(a, b):
    return jnp.dot(a, b, preferred_element_type=jnp.float32)


def layers_kernel(
    sections,
    shards,
    initial_ref,
    adjacency_ref,
    sources_ref,
    rows_ref,
    count_ref,
    weight_ref,
    out_ref,
    betas,
    tiles,
    sources,
    rows,
    count,
    weights,
    pool,
    wide,
    edge,
    tight,
    notes,
    rim_wide,
    rim_edge,
    early,
    ship_send,
    ship_recv,
    rim_send,
    rim_recv,
    near_send,
    near_recv,
    server_send,
    down_send,
    down_recv,
    up_send,
    up_recv,
    side_send,
    side_recv,
    out_send,
    out_recv,
    in_sem,
):
    z = lax.axis_index("section")
    p = lax.axis_index("node")
    span = lax.rem(z, 2)
    core = lax.rem(p, 2)
    shadow = lax.rem(p - 1 + 2 * core + shards, shards)
    sibling = p + 1 - 2 * core
    far_to = lax.rem(p + 2 - 4 * core + shards, shards)
    far_from = lax.rem(p - 2 + 4 * core + shards, shards)
    below, above = lax.rem(z + sections - 1, sections), lax.rem(z + 1, sections)
    server = z == sections - 2
    layers = jnp.where(server, sections, jnp.maximum(z + 1, 2))
    middle = sections // 2
    up_steps = middle - 1

    barrier = pltpu.get_barrier_semaphore()
    greeted = [(z, node) for node in (sibling, far_to, far_from, shadow)]
    greeted += [(below, p), (above, p)]
    for device in greeted:
        pl.semaphore_signal(barrier, inc=1, device_id=device, device_id_type=MESH)

    @pl.when((core == 1) & server)
    def _():
        pl.semaphore_signal(barrier, inc=1, device_id=(0, p), device_id_type=MESH)

    greetings = len(greeted) + jnp.where((core == 1) & (z == 0), 1, 0)

    inputs = [
        pltpu.make_async_copy(src, dst, in_sem.at[index])
        for index, (src, dst) in enumerate(
            (
                (sources_ref, sources),
                (count_ref, count),
                (rows_ref, rows),
                (initial_ref.at[span], pool.at[0, 0, ALL]),
                (adjacency_ref.at[span], tiles),
                (weight_ref.at[0], weights.at[z]),
            )
        )
    ]
    for copy in inputs:
        copy.start()

    def remote(src, dst, send, recv, device):
        return pltpu.make_async_remote_copy(
            src_ref=src,
            dst_ref=dst,
            send_sem=send,
            recv_sem=recv,
            device_id=device,
            device_id_type=MESH,
        )

    def ship(item):
        refs = (
            (notes.at[0], notes.at[1]),
            (pool.at[0, 0, ALL], pool.at[0, 1, ALL]),
            (tight.at[0], tight.at[1]),
            (edge.at[0], edge.at[1]),
        )[item]
        return remote(*refs, ship_send.at[item], ship_recv.at[item], (z, shadow))

    def rim_to_sibling(layer):
        return remote(
            pool.at[layer, 1, NEAR],
            pool.at[layer, 0, FAR],
            rim_send.at[layer, 0],
            rim_recv.at[layer, 0],
            (z, sibling),
        )

    def rim_to_far(layer):
        return remote(
            pool.at[layer, 1, NEAR],
            pool.at[layer, 1, FAR],
            rim_send.at[layer, 1],
            rim_recv.at[layer, 1],
            (z, far_to),
        )

    def rim_to_near(layer):
        return remote(
            pool.at[layer, 1, NEAR],
            pool.at[layer, 0, NEAR],
            near_send.at[layer],
            near_recv.at[layer],
            (z, shadow),
        )

    def part_of(layer, part):
        return weights.at[layer, pl.ds(part * PART, PART)]

    def to_below(layer, part):
        ref = part_of(layer, part)
        return remote(
            ref, ref, down_send.at[layer, part], down_recv.at[layer, part], (below, p)
        )

    def to_server(layer, part):
        ref = part_of(layer, part)
        there = (sections - 2, p)
        return remote(ref, ref, server_send.at[layer, part], down_recv.at[layer, part], there)

    def takes_down(layer):
        lower = (z < middle) & (layer > z) & (layer < middle)
        return (core == 1) & (lower | ((z >= middle) & (layer <= z - middle)))

    def sends_below(layer):
        lower = (z < middle) & (layer >= z) & (layer < middle)
        upper = (z > middle) & (z < sections - 1) & (layer < z - middle)
        return (core == 1) & (lower | upper)

    def sends_server(layer):
        return (core == 1) & (z == 0) & (layer < middle - 1)

    def send_down(layer, part):
        @pl.when(sends_below(layer))
        def _():
            to_below(layer, part).start()

        @pl.when(sends_server(layer))
        def _():
            to_server(layer, part).start()

    def up_copy(step, part):
        ref = part_of(lax.rem(z - step + 1 + sections, sections), part)
        at = (step - 1, part)
        return remote(ref, ref, up_send.at[at], up_recv.at[at], (above, p))

    def up_arrival(step, part):
        ref = part_of(lax.rem(z - step + sections, sections), part)
        at = (step - 1, part)
        return remote(ref, ref, up_send.at[at], up_recv.at[at], (above, p))

    def sends_up(step):
        return (step <= up_steps) & (step <= z + 1) & (z < sections - 1)

    def to_side(layer, part):
        ref = part_of(layer, part)
        return remote(
            ref, ref, side_send.at[layer, part], side_recv.at[layer, part], (z, sibling)
        )

    def relay_down(layer):
        @pl.when(takes_down(layer))
        def _():
            for part in range(PARTS):
                to_below(layer, part).wait_recv()
                send_down(layer, part)

                @pl.when(layer < layers)
                def _():
                    to_side(layer, part).start()

    def take_last():
        @pl.when((core == 1) & server)
        def _():
            for part in range(PARTS):
                to_below(z + 1, part).wait_recv()
                to_side(z + 1, part).start()

    def relay_up(step):
        @pl.when((core == 1) & (step <= up_steps) & (step <= z))
        def _():
            for part in range(PARTS):
                up_arrival(step, part).wait_recv()

                @pl.when(sends_up(step + 1))
                def _():
                    up_copy(step + 1, part).start()

                to_side(z - step, part).start()

    def have_weight(layer):
        @pl.when((core == 0) & (layer != z))
        def _():
            for part in range(PARTS):
                to_side(layer, part).wait_recv()

    def out_local():
        return pltpu.make_async_copy(pool.at[z + 1, 0, ALL], out_ref.at[0, span], out_send.at[0])

    def out_below(half):
        return remote(
            pool.at[z, 0, ALL], out_ref.at[0, half], out_send.at[1], out_recv.at[0], (below, p)
        )

    def out_above():
        return remote(
            pool.at[z + 2, 0, ALL], out_ref.at[0, span], out_send.at[2], out_recv.at[0], (above, p)
        )

    ordinals = np.arange(sections, dtype=np.float32)
    mixings = np.log(np.float32(lambda_decay) / (ordinals + np.float32(1.0)) + np.float32(1.0))
    for layer in range(sections):
        betas[layer] = jnp.float32(mixings[layer])
    for copy in inputs[:3]:
        copy.wait()
    wanted = jnp.where(span == 0, rows[0:1, :], rows[1:2, :])
    live = lax.broadcasted_iota(jnp.int32, (1, RIM), 1) < count[0, span]
    notes[0, 16:17, :] = jnp.where(live, wanted, -1).astype(jnp.float32)
    inputs[4].wait()
    for block in range(OWN):
        first = sources[span, 3 * block]
        second = sources[span, 3 * block + 1]
        third = sources[span, 3 * block + 2]
        at_before = jnp.where(second == OWN, 1, 0) + jnp.where(third == OWN, 2, 0)
        at_after = jnp.where(second == OWN + 1, 1, 0) + jnp.where(third == OWN + 1, 2, 0)
        at_own = jnp.minimum(3 - at_before - at_after, 2)
        own_tile = first + second + third - (2 * OWN + 1)
        place = pl.ds(block * TILE, TILE)
        at_far = jnp.where(core == 1, at_before, at_after)
        at_near = jnp.where(core == 1, at_after, at_before)
        edge[0, place, 0:RIM] = tiles[3 * block + at_far]
        edge[0, place, RIM : 2 * RIM] = tiles[3 * block + at_near]
        tight[0, place] = tiles[3 * block + at_own]
        for t in range(OWN):
            chosen = jnp.where(own_tile == t, 1.0, 0.0)
            notes[0, 4 * block + t : 4 * block + t + 1, :] = jnp.full((1, TILE), chosen)

    lane = lax.broadcasted_iota(jnp.int32, (RIM, TILE), 1).astype(jnp.float32)

    def picker(unit):
        turned = jnp.broadcast_to(notes[unit, 16:17, :], (RIM, RIM)).T
        return jnp.concatenate(
            [jnp.where(turned == lane + float(t * TILE), 1.0, 0.0) for t in range(OWN)], axis=1
        ).astype(jnp.bfloat16)

    def first_rim(unit):
        pool[0, 1 - unit, NEAR] = dot(picker(unit), pool[0, unit, ALL]).astype(jnp.bfloat16)

    def spread(unit):
        pick = picker(unit)
        for block in range(OWN):
            place = pl.ds(block * TILE, TILE)
            own = tight[unit, place].astype(jnp.float32)
            for t in range(OWN):
                mask = notes[unit, 4 * block + t : 4 * block + t + 1, :]
                wide[unit, place, t * TILE : (t + 1) * TILE] = (own * mask).astype(jnp.bfloat16)
        rim_wide[unit] = dot(pick, wide[unit]).astype(jnp.bfloat16)
        rim_edge[unit] = dot(pick, edge[unit]).astype(jnp.bfloat16)

    def start_rim(unit, layer):
        ready = dot(rim_wide[unit], pool[layer, unit, ALL])
        if unit == 1:
            ready += dot(rim_edge[1, :, RIM : 2 * RIM], pool[layer, 1, NEAR])
        early[unit] = ready

    def blend(aggregate, anchor):
        return (1.0 - alpha_mix) * aggregate + alpha_mix * anchor.astype(jnp.float32)

    def finish(blended, blended_b, layer):
        mixing = betas[layer]
        projected = dot(blended_b, weights[layer])
        return jnp.maximum((1.0 - mixing) * blended + mixing * projected, 0.0).astype(jnp.bfloat16)

    def rim_blend(unit, layer):
        if unit == 1:
            late = dot(rim_edge[1, :, 0:RIM], pool[layer, 1, FAR])
        else:
            late = dot(rim_edge[0], pool[layer, 0, EDGES])
        aggregate = early[unit] + late
        return blend(aggregate, pool[0, 1 - unit, NEAR])

    def end_rim(unit, layer):
        blended = rim_blend(unit, layer)
        rim = finish(blended, blended.astype(jnp.bfloat16), layer)
        pool[layer + 1, 1 - unit, NEAR] = rim

    def end_own_rim(layer):
        end_rim(0, layer)
        rim_to_far(layer + 1).start()
        rim_to_sibling(layer + 1).start()

    def all_rows(unit, layer):
        aggregate = dot(wide[unit], pool[layer, unit, ALL])
        aggregate += dot(edge[unit], pool[layer, unit, EDGES])
        blended = blend(aggregate, pool[0, unit, ALL])
        rows_b = blended.astype(jnp.bfloat16)
        pool[layer + 1, unit, ALL] = finish(blended, rows_b, layer)

    inputs[3].wait()
    first_rim(0)
    spread(0)
    inputs[5].wait()
    pl.semaphore_wait(barrier, greetings)
    for copy in (rim_to_far(0), rim_to_near(0), rim_to_sibling(0)):
        copy.start()

    @pl.when(core == 1)
    def _():
        for part in range(PARTS):
            send_down(z, part)

            @pl.when(z == sections - 1)
            def _():
                to_below(z, part).start()

            @pl.when(sends_up(1))
            def _():
                up_copy(1, part).start()

    for item in (0, 2, 3, 1):
        ship(item).start()
    start_rim(0, 0)

    def relay_down_upper(layer):
        @pl.when(z >= middle)
        def _():
            relay_down(layer)

    up_first = jnp.minimum(sections - z, up_steps)

    def relay(step, carry):
        @pl.when(z < middle)
        def _():
            relay_down(z + step)

        @pl.when(step <= up_first)
        def _():
            relay_up(step)

        return carry

    lax.fori_loop(1, middle, relay, 0)
    relay_down_upper(0)
    have_weight(0)
    rim_to_sibling(0).wait_recv()
    rim_to_near(0).wait_recv()
    end_own_rim(0)
    rim_to_near(1).start()
    all_rows(0, 0)
    start_rim(0, 1)
    relay_down_upper(1)
    take_last()
    have_weight(1)
    rim_to_sibling(1).wait_recv()
    rim_to_near(1).wait_recv()

    @pl.when(layers > 2)
    def _():
        end_own_rim(1)

    all_rows(0, 1)
    relay_down_upper(2)
    ship(0).wait_recv()
    ship(2).wait_recv()
    ship(3).wait_recv()
    spread(1)
    ship(1).wait_recv()
    rim_to_far(0).wait_recv()

    @pl.when(layers > 2)
    def _():
        start_rim(0, 2)
        all_rows(1, 0)
        start_rim(1, 1)

    def step(i, carry):
        @pl.when(i == z - 1)
        def _():
            out_below(span).start()

        @pl.when(i == z)
        def _():
            out_local().start()

        rim_to_far(i).wait_recv()
        end_rim(1, i)
        have_weight(i + 1)
        rim_to_sibling(i + 1).wait_recv()

        @pl.when(i < layers - 2)
        def _():
            end_own_rim(i + 1)

            relay_up(up_first + i)
            all_rows(1, i)
            start_rim(1, i + 1)
            relay_down_upper(i + 2)

        all_rows(0, i + 1)

        @pl.when(i < layers - 2)
        def _():
            start_rim(0, i + 2)

        return carry

    lax.fori_loop(1, layers - 1, step, 0)

    @pl.when(z == 1)
    def _():
        out_below(span).start()

    @pl.when(server)
    def _():
        out_above().start()

    @pl.when(jnp.logical_not(server))
    def _():
        out_local().start()

    for item in range(4):
        ship(item).wait_send()
    for layer in range(2):
        rim_to_near(layer).wait_send()

    def sent(layer, carry):
        rim_to_sibling(layer).wait_send()
        rim_to_far(layer).wait_send()

        @pl.when((core == 1) & (layer != z))
        def _():
            for part in range(PARTS):
                to_side(layer, part).wait_send()

        return carry

    lax.fori_loop(0, layers, sent, 0)
    rim_to_far(layers - 1).wait_recv()

    @pl.when(core == 1)
    def _():
        for part in range(PARTS):
            for layer in range(middle):

                @pl.when(sends_below(layer))
                def _():
                    to_below(layer, part).wait_send()

                @pl.when(sends_server(layer))
                def _():
                    to_server(layer, part).wait_send()

            @pl.when(z == sections - 1)
            def _():
                to_below(z, part).wait_send()

            for step in range(1, up_steps + 1):

                @pl.when(sends_up(step))
                def _():
                    up_copy(step, part).wait_send()

    out_local().wait()

    @pl.when(z > 0)
    def _():
        out_below(span).wait_send()

    @pl.when(server)
    def _():
        out_above().wait_send()

    out_below(1 - span).wait_recv()


def solution(mesh):
    sections, shards = mesh.shape["section"], mesh.shape["node"]

    def on_device(initial, adjacency, sources, boundary_rows, boundary_count, layer_weights):
        def body(*refs):
            layers_kernel(sections, shards, *refs)

        dma = pltpu.SemaphoreType.DMA
        middle = sections // 2
        return pl.pallas_call(
            body,
            out_shape=jax.ShapeDtypeStruct((1, SPANS, ROWS, WIDTH), jnp.bfloat16),
            in_specs=[pl.BlockSpec(memory_space=pltpu.HBM)] * 6,
            out_specs=pl.BlockSpec(memory_space=pltpu.HBM),
            scratch_shapes=[
                pltpu.SMEM((sections,), jnp.float32),
                pltpu.VMEM((OWN * 3, TILE, TILE), jnp.bfloat16),
                pltpu.SMEM((SPANS, OWN * 3), jnp.int32),
                pltpu.VMEM((SPANS, RIM), jnp.int32),
                pltpu.SMEM((1, SPANS), jnp.int32),
                pltpu.VMEM((sections, WIDTH, WIDTH), jnp.bfloat16),
                pltpu.VMEM((sections + 1, 2, POOL, WIDTH), jnp.bfloat16),
                pltpu.VMEM((2, ROWS, ROWS), jnp.bfloat16),
                pltpu.VMEM((2, ROWS, 2 * RIM), jnp.bfloat16),
                pltpu.VMEM((2, ROWS, TILE), jnp.bfloat16),
                pltpu.VMEM((2, NOTES, TILE), jnp.float32),
                pltpu.VMEM((2, RIM, ROWS), jnp.bfloat16),
                pltpu.VMEM((2, RIM, 2 * RIM), jnp.bfloat16),
                pltpu.VMEM((2, RIM, WIDTH), jnp.float32),
                dma((4,)),
                dma((4,)),
                dma((sections, 2)),
                dma((sections, 2)),
                dma((2,)),
                dma((2,)),
                dma((middle, PARTS)),
                dma((sections, PARTS)),
                dma((sections, PARTS)),
                dma((middle, PARTS)),
                dma((middle, PARTS)),
                dma((sections, PARTS)),
                dma((sections, PARTS)),
                dma((3,)),
                dma((1,)),
                dma((6,)),
            ],
            compiler_params=pltpu.CompilerParams(
                collective_id=0, has_side_effects=True, vmem_limit_bytes=60 * 1024 * 1024
            ),
        )(
            initial,
            adjacency,
            sources,
            boundary_rows,
            boundary_count.reshape(1, SPANS),
            layer_weights,
        )

    in_specs = (
        P(None, "node", None),
        P(None, "node", None, None),
        P(None, "node"),
        P(None, "node"),
        P(None, "node"),
        P("section", None, None),
    )
    out_specs = P("section", None, "node", None)
    return jax.shard_map(
        on_device, mesh=mesh, in_specs=in_specs, out_specs=out_specs, check_vma=False
    )
```
